128 devices in a mesh: tensor: 4 (over y), ctx: 16 (over x_hi, z, core), section: 2 (over x_lo).
Axes of the slice: x: 4 (x_hi: 2, x_lo: 2; x = x_hi * 2 + x_lo), y: 4, z: 4, core: 2. Of those that a mesh axis runs over, the one named last changes fastest.
Arguments:
- segment_query: bfloat16 [4096, 8192], P('ctx', ('tensor', 'section')), may hold values from -64 to 64
- segment_key_value: bfloat16 [4096, 2048], P('ctx', ('tensor', 'section')), may hold values from -64 to 64
- earlier_key_value: bfloat16 [4096, 2048], P('ctx', ('tensor', 'section')), may hold values from -6 to 6
- fill_start: int32 [1], replicated, may hold values from 2048 to 4096
- block_page: int32 [64], replicated, may hold values from 0 to 63, each once
- decode_query: bfloat16 [256, 4, 8192], P('ctx', None, ('tensor', 'section')), may hold values from -64 to 64
- decode_key_value: bfloat16 [256, 4, 2048], P('ctx', None, ('tensor', 'section')), may hold values from -64 to 64
- cached_key_value: bfloat16 [256, 1024, 2048], P(('ctx', 'section'), None, 'tensor'), may hold values from -6 to 6
- cache_length: int32 [256], P(('ctx', 'section')), may hold values from 1 to 1024, 131072 in all
Outputs:
- fill_output: bfloat16 [4096, 8192], P('ctx', ('tensor', 'section'))
- shipped_pages: bfloat16 [64, 64, 2048], P(('ctx', 'section'), None, 'tensor')
- step_output: bfloat16 [256, 4, 8192], P(('ctx', 'section'), None, 'tensor')
The draws below stay inside these ranges and needn't reach their ends.
Inputs may be any that keep to these rules, and one draw needn't show every extreme that they name: `block_page`: each page is named by exactly one block. `cache_length`: some row has exactly 1024.
All inputs are finite; a program needn't handle non-finite values. No bound on the sum of `cache_length` on one device may be relied on, other than what follows from the above.
Results may differ from the reference program's by a relative error of at most 0.01.
Values may be sent and summed in bfloat16 or wider, within the bound.
A program may use at most 128 MiB of HBM per device.

```python
import math
import jax
import jax.numpy as jnp
import numpy as np
from jax import lax

QUERY_HEADS = 64
KEYVALUE_HEADS = 8
HEAD_SIZE = 128
PAGE_TOKENS = 64
CACHE_SLOTS = 1024
NEW_TOKENS = 4
SEGMENT_TOKENS = 4096
EARLIER_SLOTS = 4096
SEGMENT_PAGES = 64
DECODE_ROWS = 256


theta_base = 500000.0


def turn_vectors(vectors, position):
    half_width = vectors.shape[-1] // 2
    frequency = theta_base ** (-(jnp.arange(half_width).astype(jnp.float32) * 2.0 / vectors.shape[-1]))
    angles = position[..., None] * frequency
    cosine = jnp.cos(angles)
    sine_part = jnp.sin(angles)
    first_half = vectors[..., :half_width]
    second_half = vectors[..., half_width:]
    return jnp.concatenate([first_half * cosine - second_half * sine_part, second_half * cosine + first_half * sine_part], -1)


def base_parts(key, leading_part, strength):
    key_value_pair, query_key_scores, key_scale, key_pick, key_level = jax.random.split(key, 5)
    base_data = jax.random.normal(key_value_pair, leading_part + (KEYVALUE_HEADS, 2, HEAD_SIZE), jnp.float32)
    spread = jnp.exp(strength * jax.random.uniform(key_scale, leading_part + (1, 1, 1), jnp.float32, 0.0, 0.7))
    query_vectors = jax.random.normal(query_key_scores, leading_part + (KEYVALUE_HEADS, QUERY_HEADS // KEYVALUE_HEADS, HEAD_SIZE), jnp.float32)
    picked = jax.random.randint(key_pick, leading_part + (1, 1, 1), 0, 48) == 0
    levels = jax.random.randint(key_level, leading_part + (1, 1, 1), 3, 6).astype(jnp.float32) * (4.0 * strength)
    return (base_data, spread, query_vectors, picked, levels)


def finish_parts(base_data, spread, query_vectors, picked, levels, aligned):
    key_value_data = base_data * spread
    query_vectors = jnp.where(picked & (levels > 0.0), levels * aligned[..., None, :], query_vectors)
    return (jnp.clip(query_vectors, -64.0, 64.0), jnp.clip(key_value_data, -64.0, 64.0))


def segment_heads(key, strength):
    base_data, spread, query_vectors, picked, levels = base_parts(key, (SEGMENT_TOKENS,), strength)
    token_index = jnp.arange(SEGMENT_TOKENS, dtype=jnp.int32)
    source_index = jax.random.randint(jax.random.fold_in(key, 7), (SEGMENT_TOKENS,), jnp.zeros((SEGMENT_TOKENS,), jnp.int32), token_index + 1)
    offsets = (source_index - token_index).astype(jnp.float32)
    aligned = turn_vectors(base_data[source_index][:, :, 0], offsets[:, None])
    picked = picked & (token_index >= 1)[:, None, None, None]
    return finish_parts(base_data, spread, query_vectors, picked, levels, aligned)


def decode_heads(key, strength):
    base_data, spread, query_vectors, picked, levels = base_parts(key, (DECODE_ROWS, NEW_TOKENS), strength)
    step_index = jnp.arange(NEW_TOKENS, dtype=jnp.int32)
    offsets = -step_index.astype(jnp.float32)
    aligned = turn_vectors(base_data[:, 0:1, :, 0], offsets[None, :, None])
    picked = picked & (step_index >= 1)[None, :, None, None, None]
    return finish_parts(base_data, spread, query_vectors, picked, levels, aligned)


def draw_segment_query(key, part):
    query_vectors, key_value_data = segment_heads(jax.random.fold_in(key, 101), 0.0)
    return query_vectors.reshape(SEGMENT_TOKENS, QUERY_HEADS * HEAD_SIZE).astype(jnp.bfloat16)


def draw_segment_key_value(key, part):
    query_vectors, key_value_data = segment_heads(jax.random.fold_in(key, 101), 0.0)
    return key_value_data.reshape(SEGMENT_TOKENS, KEYVALUE_HEADS * 2 * HEAD_SIZE).astype(jnp.bfloat16)


def draw_decode_query(key, part):
    query_vectors, key_value_data = decode_heads(jax.random.fold_in(key, 202), 0.0)
    return query_vectors.reshape(DECODE_ROWS, NEW_TOKENS, QUERY_HEADS * HEAD_SIZE).astype(jnp.bfloat16)


def draw_decode_key_value(key, part):
    query_vectors, key_value_data = decode_heads(jax.random.fold_in(key, 202), 0.0)
    return key_value_data.reshape(DECODE_ROWS, NEW_TOKENS, KEYVALUE_HEADS * 2 * HEAD_SIZE).astype(jnp.bfloat16)


def block_scale(own_key, dims, shards, least, largest):
    gain = 1.0
    for dim, blocks in shards:
        draws = jax.random.uniform(jax.random.fold_in(jax.random.fold_in(own_key, 6), dim), (blocks,), jnp.float32, least / len(shards), largest / len(shards))
        gain = gain * jnp.repeat(jnp.exp(draws), dims[dim] // blocks).reshape((-1,) + (1,) * (len(dims) - 1 - dim))
    return gain


def length_profile(amount, total, bound, skew):
    loads = [(1 << 20) // math.isqrt(standing ** skew) + 1 for standing in range(2, amount + 1)]
    surplus, holding = total - bound - (amount - 1), [1] * (amount - 1)
    while surplus > 0:
        candidates = [i for i in range(amount - 1) if holding[i] < bound]
        whole, left = sum([loads[i] for i in candidates]), surplus
        for i in candidates:
            extra = min(bound - holding[i], max(1, left * loads[i] // whole), surplus)
            holding[i] = holding[i] + extra
            surplus = surplus - extra
    return np.array([bound] + holding)


def ragged(key, amount, total, most, slope):
    if amount == 2:
        one = jax.random.randint(key, (), max(1, total - most), min(most, total - 1) + 1)
        return jnp.stack([one, total - one])
    lengths = jnp.asarray(length_profile(amount, total, most, slope), jnp.int32)
    pairs = (amount - 1) // 2
    donor, sink = lengths[1:1 + 2 * pairs:2], lengths[2:2 + 2 * pairs:2]
    slack = jnp.minimum(donor - 1, most - sink)
    shifted = jax.random.randint(jax.random.fold_in(key, 1), (pairs,), 0, 1 << 20) % (slack + 1)
    lengths = lengths.at[1:1 + 2 * pairs:2].set(donor - shifted).at[2:2 + 2 * pairs:2].set(sink + shifted)
    return lengths[jax.random.permutation(jax.random.fold_in(key, 2), amount)]


def gaussian(own_key, extent, scale, limit, cuts=(), kind=jnp.bfloat16):
    factor_of = block_scale(own_key, extent, cuts, -0.22, 0.18) if cuts else 1.0
    entries = jax.random.normal(own_key, extent, jnp.float32) * scale * factor_of
    return jnp.minimum(jnp.maximum(entries, -limit), limit).astype(kind)


def setup_inputs(seed: int = 0) -> dict:
    splits = jax.random.split(jax.random.key(seed), 10)
    segment_query = draw_segment_query(jax.random.fold_in(splits[9], 71), 0)
    segment_key_value = draw_segment_key_value(jax.random.fold_in(splits[9], 71), 0)
    earlier_key_value = gaussian(splits[2], (EARLIER_SLOTS, KEYVALUE_HEADS * 2 * HEAD_SIZE), 1.0, 6.0, ((0, 16), (1, 8)))
    fill_start = jax.random.randint(splits[3], (1,), EARLIER_SLOTS // 2, EARLIER_SLOTS + 1).astype(jnp.int32)
    block_page = jax.random.permutation(splits[4], SEGMENT_PAGES).astype(jnp.int32)
    decode_query = draw_decode_query(jax.random.fold_in(splits[9], 71), 0)
    decode_key_value = draw_decode_key_value(jax.random.fold_in(splits[9], 71), 0)
    cached_key_value = gaussian(splits[7], (DECODE_ROWS, CACHE_SLOTS, KEYVALUE_HEADS * 2 * HEAD_SIZE), 1.0, 6.0, ((0, 32), (2, 4)))
    cache_length = ragged(splits[8], DECODE_ROWS, DECODE_ROWS * CACHE_SLOTS // 2, CACHE_SLOTS, 2).astype(jnp.int32)
    return dict(segment_query=segment_query, segment_key_value=segment_key_value, earlier_key_value=earlier_key_value, fill_start=fill_start, block_page=block_page, decode_query=decode_query, decode_key_value=decode_key_value, cached_key_value=cached_key_value, cache_length=cache_length)


theta_base = 500000.0
neg_big = -1e+30

def apply_rotary(vectors, position):
    half_width = vectors.shape[-1] // 2
    frequency = theta_base ** (-(jnp.arange(half_width).astype(jnp.float32) * 2.0 / vectors.shape[-1]))
    angles = position[..., None] * frequency
    cosine = jnp.cos(angles)
    sine_part = jnp.sin(angles)
    first_half = vectors[..., :half_width]
    second_half = vectors[..., half_width:]
    return jnp.concatenate([first_half * cosine - second_half * sine_part, second_half * cosine + first_half * sine_part], -1)

def reference(segment_query, segment_key_value, earlier_key_value, fill_start, block_page, decode_query, decode_key_value, cached_key_value, cache_length):
    query_group_count = QUERY_HEADS // KEYVALUE_HEADS
    score_scale = 1.0 / math.sqrt(HEAD_SIZE)
    start_pos = fill_start[0]
    token_positions = start_pos + jnp.arange(SEGMENT_TOKENS, dtype=jnp.int32)
    rotated_queries = apply_rotary(segment_query.astype(jnp.float32).reshape(SEGMENT_TOKENS, KEYVALUE_HEADS, query_group_count, HEAD_SIZE), token_positions[:, None, None].astype(jnp.float32)).astype(jnp.bfloat16)
    fresh_entries = segment_key_value.reshape(SEGMENT_TOKENS, KEYVALUE_HEADS, 2, HEAD_SIZE)
    rotated_keys = apply_rotary(fresh_entries[:, :, 0].astype(jnp.float32), token_positions[:, None].astype(jnp.float32)).astype(jnp.bfloat16)
    finished_rows = jnp.stack([rotated_keys, fresh_entries[:, :, 1]], 2).reshape(SEGMENT_TOKENS, KEYVALUE_HEADS * 2 * HEAD_SIZE)
    page_listing = finished_rows.reshape(SEGMENT_PAGES, PAGE_TOKENS, KEYVALUE_HEADS * 2 * HEAD_SIZE)
    shipped_pages = jnp.zeros_like(page_listing).at[block_page].set(page_listing)
    earlier_part = earlier_key_value.reshape(EARLIER_SLOTS, KEYVALUE_HEADS, 2, HEAD_SIZE)
    context_keys = jnp.concatenate([earlier_part[:, :, 0], rotated_keys], 0)
    context_values = jnp.concatenate([earlier_part[:, :, 1], fresh_entries[:, :, 1]], 0)
    prior_index = jnp.arange(EARLIER_SLOTS, dtype=jnp.int32)
    key_pos = jnp.concatenate([prior_index, token_positions], 0)
    key_usable = jnp.concatenate([prior_index < start_pos, jnp.ones((SEGMENT_TOKENS,), bool)], 0)
    query_row_data = math.gcd(SEGMENT_TOKENS, 512)
    query_pages = rotated_queries.reshape(SEGMENT_TOKENS // query_row_data, query_row_data, KEYVALUE_HEADS, query_group_count, HEAD_SIZE)
    pos_blocks = token_positions.reshape(SEGMENT_TOKENS // query_row_data, query_row_data)

    def per_block(packed):
        block_query, block_pos = packed
        allowed = (key_pos[None, :] <= block_pos[:, None]) & key_usable[None, :]

        def per_head(head_packed):
            head_query, head_keys, head_values = head_packed
            scores = jnp.einsum('tgd,sd->tgs', head_query.astype(jnp.float32), head_keys.astype(jnp.float32)) * score_scale
            scores = jnp.where(allowed[:, None, :], scores, neg_big)
            row_max = lax.optimization_barrier(jnp.max(scores, -1, keepdims=True))
            weights = jnp.where(allowed[:, None, :], jnp.exp(scores - row_max), 0.0)
            weight_sum = lax.optimization_barrier(jnp.sum(weights, -1, keepdims=True))
            rounded = lax.optimization_barrier(weights.astype(jnp.bfloat16)).astype(jnp.float32)
            mixed = jnp.einsum('tgs,sd->tgd', rounded, head_values.astype(jnp.float32))
            return (mixed / weight_sum).astype(jnp.bfloat16)
        heads_out = lax.map(per_head, (jnp.moveaxis(block_query, 1, 0), jnp.moveaxis(context_keys, 1, 0), jnp.moveaxis(context_values, 1, 0)))
        return jnp.moveaxis(heads_out, 0, 1)
    fill_output = lax.map(per_block, (query_pages, pos_blocks)).reshape(SEGMENT_TOKENS, QUERY_HEADS * HEAD_SIZE)
    decode_positions = cache_length[:, None] + jnp.arange(NEW_TOKENS, dtype=jnp.int32)[None, :]
    decode_rotated = apply_rotary(decode_query.astype(jnp.float32).reshape(DECODE_ROWS, NEW_TOKENS, KEYVALUE_HEADS, query_group_count, HEAD_SIZE), decode_positions[:, :, None, None].astype(jnp.float32)).astype(jnp.bfloat16)
    decode_fresh_entries = decode_key_value.reshape(DECODE_ROWS, NEW_TOKENS, KEYVALUE_HEADS, 2, HEAD_SIZE)
    step_key = apply_rotary(decode_fresh_entries[:, :, :, 0].astype(jnp.float32), decode_positions[:, :, None].astype(jnp.float32)).astype(jnp.bfloat16)
    step_values = decode_fresh_entries[:, :, :, 1]
    cache_entries = cached_key_value.reshape(DECODE_ROWS, CACHE_SLOTS, KEYVALUE_HEADS, 2, HEAD_SIZE)
    slot_index = jnp.arange(CACHE_SLOTS, dtype=jnp.int32)
    step_index = jnp.arange(NEW_TOKENS, dtype=jnp.int32)
    new_ok = step_index[None, :] <= step_index[:, None]

    def per_row(packed):
        row_query, row_keys, row_values, row_cache, row_length = packed
        old_ok = slot_index < row_length
        old_scores = jnp.einsum('jhgd,chd->jhgc', row_query.astype(jnp.float32), row_cache[:, :, 0].astype(jnp.float32)) * score_scale
        new_scores = jnp.einsum('jhgd,khd->jhgk', row_query.astype(jnp.float32), row_keys.astype(jnp.float32)) * score_scale
        old_scores = jnp.where(old_ok[None, None, None, :], old_scores, neg_big)
        new_scores = jnp.where(new_ok[:, None, None, :], new_scores, neg_big)
        row_max = jnp.maximum(lax.optimization_barrier(jnp.max(old_scores, -1, keepdims=True)), lax.optimization_barrier(jnp.max(new_scores, -1, keepdims=True)))
        old_weights = jnp.where(old_ok[None, None, None, :], jnp.exp(old_scores - row_max), 0.0)
        new_weights = jnp.where(new_ok[:, None, None, :], jnp.exp(new_scores - row_max), 0.0)
        weight_sum = lax.optimization_barrier(jnp.sum(old_weights, -1, keepdims=True)) + lax.optimization_barrier(jnp.sum(new_weights, -1, keepdims=True))
        old_rounded = lax.optimization_barrier(old_weights.astype(jnp.bfloat16)).astype(jnp.float32)
        new_rounded = lax.optimization_barrier(new_weights.astype(jnp.bfloat16)).astype(jnp.float32)
        mixed = jnp.einsum('jhgc,chd->jhgd', old_rounded, row_cache[:, :, 1].astype(jnp.float32))
        mixed = mixed + jnp.einsum('jhgk,khd->jhgd', new_rounded, row_values.astype(jnp.float32))
        return (mixed / weight_sum).astype(jnp.bfloat16)
    step_output = lax.map(per_row, (decode_rotated, step_key, step_values, cache_entries, cache_length)).reshape(DECODE_ROWS, NEW_TOKENS, QUERY_HEADS * HEAD_SIZE)
    return (fill_output, shipped_pages, step_output)
```

```python
import functools
import math

import jax
import jax.numpy as jnp
import numpy as np
from jax import lax
from jax.experimental import pallas as pl
from jax.experimental.pallas import tpu as pltpu
from jax.sharding import PartitionSpec as P

HEAD = 128
GROUP = 8
PAGE = 64
TOK = 256
CHIP = 4 * TOK
ROWS = 8
STEPS = 4
SLOTS = 1024
BLOCK = 512
NEG = -1e30
FAR = 1 << 30
SCALE = math.log2(math.e) / math.sqrt(HEAD)
THETA = 500000.0
MESH = pl.DeviceIdType.MESH
NT = (((1,), (1,)), ((), ()))


def mm(a, b):
    return jnp.dot(a, b, preferred_element_type=jnp.float32)


def mm_nt(a, b):
    return lax.dot_general(a, b, NT, preferred_element_type=jnp.float32)


def rotate(x, cosine, sine):
    return x * cosine + pltpu.roll(x, 64, 1) * sine


def kernel(
    sq_hbm, skv_hbm, ekv_hbm, start_ref, page_ref, dq_hbm, dkv_hbm, cache_hbm, len_ref,
    cos_ref, sin_ref, freq_ref,
    fill_ref, pages_ref, step_ref,
    near_keys, far_keys, sq, skv, qs, acc, top, bias, scores, dq, dkv, cache, qd, od, d_top, d_total, d_acc,
    page_out, page_in,
    load_sem, cache_sem, c_send, c_recv, s_send, s_recv,
    d_send, d_recv, p_send, p_recv,
):
    ctx = lax.axis_index("ctx")
    sec = lax.axis_index("section")
    core = ctx % 2
    z = (ctx // 2) % 4
    x = ctx // 8
    sibling = {"ctx": x * 8 + z * 2 + 1 - core}
    partner = {"section": 1 - sec}
    start = start_ref[0]

    def chip_of(dx, dz):
        column = x if dx == 0 else 1 - x
        return column * 4 + (z + dz) % 4

    near = ((0, 0), (1, 0), (0, 1), (0, 3))
    far = ((1, 1), (1, 3), (0, 2), (1, 2))

    def place(dx, dz, piece, other_core=0):
        ref, ways = (near_keys, near) if (dx, dz) in near else (far_keys, far)
        return ref.at[pl.ds(ways.index((dx, dz)) * CHIP + (2 * piece + other_core) * TOK, TOK)]

    def remote(src, dst, send, recv, device):
        return pltpu.make_async_remote_copy(
            src_ref=src, dst_ref=dst, send_sem=send, recv_sem=recv,
            device_id=device, device_id_type=MESH,
        )

    def peer(dx, dz):
        return {"ctx": chip_of(dx, dz) * 2 + core}

    def chip_copy(piece, dx, dz):
        back = (4 - dz) % 4
        return remote(
            place(0, 0, piece), place(dx, back, piece),
            c_send.at[piece, dx, dz], c_recv.at[piece, dx, back], peer(dx, dz),
        )

    def chip_arrival(piece, dx, dz):
        ref = place(dx, dz, piece)
        return remote(ref, ref, c_send.at[piece, dx, dz], c_recv.at[piece, dx, dz], peer(dx, dz))

    def core_copy(piece, dx, dz):
        return remote(
            place(dx, dz, piece), place(dx, dz, piece, 1),
            s_send.at[piece, dx, dz], s_recv.at[piece, dx, dz], sibling,
        )

    def pass_on(ways):
        for dx, dz in ways:
            for piece in (0, 1):
                chip_arrival(piece, dx, dz).wait_recv()
                core_copy(piece, dx, dz).start()

    def from_sibling(ways):
        for dx, dz in ways:
            for piece in (0, 1):
                core_copy(piece, dx, dz).wait_recv()

    barrier = pltpu.get_barrier_semaphore()
    for device in [peer(dx, dz) for dx, dz in near[1:] + far] + [sibling, partner]:
        pl.semaphore_signal(barrier, inc=1, device_id=device, device_id_type=MESH)

    load_e = pltpu.make_async_copy(ekv_hbm, place(0, 0, 0), load_sem.at[0])
    load_kv = pltpu.make_async_copy(skv_hbm, skv, load_sem.at[1])
    load_q = pltpu.make_async_copy(sq_hbm, sq, load_sem.at[2])
    load_e.start()
    load_kv.start()
    load_q.start()
    mine = pl.ds(sec * ROWS, ROWS)
    other = pl.ds((1 - sec) * ROWS, ROWS)
    load_dq = pltpu.make_async_copy(dq_hbm.at[mine], dq.at[sec], load_sem.at[3])
    load_dkv = pltpu.make_async_copy(dkv_hbm.at[mine], dkv.at[sec], load_sem.at[4])
    load_dq.start()
    load_dkv.start()

    def cache_copy(row):
        return pltpu.make_async_copy(cache_hbm.at[row], cache.at[row], cache_sem.at[row])

    for row in range(ROWS):
        cache_copy(row).start()

    lane = lax.broadcasted_iota(jnp.int32, (1, HEAD), 1)
    sign = jnp.where(lane < HEAD // 2, -1.0, 1.0)
    freq = freq_ref[0:1, :]
    first_angle = (start + ctx * TOK).astype(jnp.float32) * freq_ref[...]
    base_cos = jnp.cos(first_angle)[0:1]
    base_sin = jnp.sin(first_angle)[0:1]
    cosine = cos_ref[...] * base_cos - sin_ref[...] * base_sin
    sine = (sin_ref[...] * base_cos + cos_ref[...] * base_sin) * sign

    load_kv.wait()
    turned = rotate(skv[:, :HEAD].astype(jnp.float32), cosine, sine).astype(jnp.bfloat16)
    fresh_rows = slice(2 * TOK, 3 * TOK)
    near_keys[fresh_rows, :HEAD] = turned
    near_keys[fresh_rows, HEAD:] = skv[:, HEAD:]

    load_e.wait()
    pl.semaphore_wait(barrier, 9)
    send_dq = remote(dq_hbm.at[other], dq.at[sec], d_send.at[0], d_recv.at[0], partner)
    send_dkv = remote(dkv_hbm.at[other], dkv.at[sec], d_send.at[1], d_recv.at[1], partner)
    for piece in (0, 1):
        for dx, dz in near[1:]:
            chip_copy(piece, dx, dz).start()
        core_copy(piece, 0, 0).start()
        if piece == 0:
            send_dkv.start()
            send_dq.start()

    load_q.wait()
    for g in range(GROUP):
        part = sq[:, g * HEAD : (g + 1) * HEAD].astype(jnp.float32)
        scaled = rotate(part, cosine, sine).astype(jnp.bfloat16).astype(jnp.float32) * SCALE
        high = scaled.astype(jnp.bfloat16)
        low = (scaled - high.astype(jnp.float32)).astype(jnp.bfloat16)
        qs[g * TOK : (g + 1) * TOK, :] = jnp.concatenate([high, low], 1)

    load_dq.wait()
    load_dkv.wait()
    remote(dkv_hbm.at[other], dkv.at[1 - sec], d_send.at[1], d_recv.at[1], partner).wait_recv()
    remote(dq_hbm.at[other], dq.at[1 - sec], d_send.at[0], d_recv.at[0], partner).wait_recv()
    line = lax.broadcasted_iota(jnp.int32, (ROWS * STEPS, HEAD), 0)
    position = line % STEPS
    for row in range(ROWS):
        position = position + jnp.where(line // STEPS == row, len_ref[row], 0)
    angle = position.astype(jnp.float32) * freq
    step_cos = jnp.cos(angle)
    step_sin = jnp.sin(angle) * sign
    count = ROWS * STEPS * GROUP
    to_line = lax.broadcasted_iota(jnp.int32, (count, count), 0)
    from_line = lax.broadcasted_iota(jnp.int32, (count, count), 1)
    per_row = STEPS * GROUP
    wanted = (
        (to_line // STEPS) % GROUP * (ROWS * STEPS)
        + to_line // per_row * STEPS
        + to_line % STEPS
    )
    permute = jnp.where(wanted == from_line, 1.0, 0.0).astype(jnp.bfloat16)
    q_line = lax.broadcasted_iota(jnp.int32, (count, ROWS * STEPS), 0)
    k_line = lax.broadcasted_iota(jnp.int32, (count, ROWS * STEPS), 1)
    fresh_ok = (q_line // per_row == k_line // STEPS) & (k_line % STEPS <= q_line % STEPS)
    slot = lax.broadcasted_iota(jnp.int32, (1, SLOTS), 1)
    for h in range(2):
        lines = dq[h].astype(jnp.float32).reshape(ROWS * STEPS, GROUP * HEAD)
        parts = [
            rotate(lines[:, g * HEAD : (g + 1) * HEAD], step_cos, step_sin)
            for g in range(GROUP)
        ]
        ordered = mm(permute, jnp.concatenate(parts, 0).astype(jnp.bfloat16))
        ordered = ordered.astype(jnp.bfloat16)
        qd[h] = ordered
        fresh = dkv[h].astype(jnp.float32).reshape(ROWS * STEPS, 2 * HEAD)
        step_key = rotate(fresh[:, :HEAD], step_cos, step_sin).astype(jnp.bfloat16)
        s = jnp.where(fresh_ok, mm_nt(ordered, step_key) * SCALE, NEG)
        m = jnp.max(s, -1, keepdims=True)
        p = jnp.exp2(s - m)
        d_top[h] = m
        d_total[h] = jnp.sum(p, -1, keepdims=True)
        d_acc[h] = mm(p.astype(jnp.bfloat16), fresh[:, HEAD:].astype(jnp.bfloat16))

    def decode_row(row, carry):
        mask = slot < len_ref[row]
        lines = pl.ds(pl.multiple_of(row * per_row, per_row), per_row)
        for h in range(2):
            m0, l0, a0 = d_top[h, lines, :], d_total[h, lines, :], d_acc[h, lines, :]
            s = mm_nt(qd[h, lines, :], cache[row, :, h * 256 : h * 256 + 128])
            s = jnp.where(mask, s * SCALE, NEG)
            m = jnp.maximum(m0, jnp.max(s, -1, keepdims=True))
            p = jnp.exp2(s - m)
            factor = jnp.exp2(m0 - m)
            weight = l0 * factor + jnp.sum(p, -1, keepdims=True)
            mixed = a0 * factor + mm(
                p.astype(jnp.bfloat16), cache[row, :, h * 256 + 128 : (h + 1) * 256]
            )
            od[h, lines, :] = (mixed / weight).astype(jnp.bfloat16)
        return carry

    for row in range(ROWS):
        cache_copy(row).wait()
    lax.fori_loop(0, ROWS // 2, decode_row, 0)
    for piece in (0, 1):
        for dx, dz in far:
            chip_copy(piece, dx, dz).start()
    pass_on(near[1:])
    lax.fori_loop(ROWS // 2, ROWS, decode_row, 0)
    for h in range(2):
        back = lax.dot_general(
            permute, od[h], (((0,), (0,)), ((), ())), preferred_element_type=jnp.float32
        )
        for g in range(GROUP):
            lines = back[g * ROWS * STEPS : (g + 1) * ROWS * STEPS]
            lanes = slice((h * GROUP + g) * HEAD, (h * GROUP + g + 1) * HEAD)
            step_ref[:, :, lanes] = lines.reshape(ROWS, STEPS, HEAD).astype(jnp.bfloat16)

    key_lane = lax.broadcasted_iota(jnp.int32, (1, CHIP), 1)
    in_core = key_lane % (2 * TOK) // TOK
    in_chip = (core + in_core - 2 * core * in_core) * TOK + key_lane % TOK
    own_chip = chip_of(0, 0)
    for i, way in enumerate(near + far):
        chip = chip_of(*way)
        earlier = jnp.where(chip * 2 * TOK + in_chip < start, 0.0, NEG)
        fresh = jnp.where(own_chip >= chip, 0.0, NEG)
        bias[i : i + 1, :] = jnp.where(key_lane < 2 * TOK, earlier, fresh)
    own_limit = jnp.where(key_lane < 2 * TOK, -1, own_chip * 2 * TOK + in_chip)
    token = ctx * TOK + lax.broadcasted_iota(jnp.int32, (BLOCK, 1), 0) % TOK
    ones = jnp.ones((CHIP, HEAD), jnp.bfloat16)
    blocks = GROUP * TOK // BLOCK

    def lines_of(block):
        return pl.ds(pl.multiple_of(block * BLOCK, BLOCK), BLOCK)

    def score(block, part, i):
        key = (near_keys, far_keys)[part][i * CHIP : (i + 1) * CHIP, :HEAD]
        s = mm_nt(qs[lines_of(block), :], jnp.concatenate([key, key], 1))
        s = s + bias[part * 4 + i : part * 4 + i + 1, :]
        return jnp.where(own_limit <= token, s, NEG) if part == 0 and i == 0 else s

    def step(part, block, carry):
        lines = lines_of(block)
        m, a = top[lines, :], acc[lines, :]
        s = scores[...]
        for i in range(4):
            if i < 3:
                following = score(block, part, i + 1)
            else:
                scores[...] = score((block + 1) % blocks, part, 0)
            higher = jnp.maximum(m, jnp.max(s, -1, keepdims=True))
            p = jnp.exp2(s - higher)
            values = (near_keys, far_keys)[part][i * CHIP : (i + 1) * CHIP, HEAD:]
            a = a * jnp.exp2(m - higher) + mm(
                p.astype(jnp.bfloat16), jnp.concatenate([values, ones], 1)
            )
            m = higher
            s = following
        top[lines, :], acc[lines, :] = m, a
        return carry

    from_sibling(near)
    acc[...] = jnp.zeros_like(acc)
    top[...] = jnp.full_like(top, NEG)
    scores[...] = score(0, 0, 0)
    lax.fori_loop(0, blocks, functools.partial(step, 0), 0)

    pass_on(far)
    from_sibling(far)

    own_page = (ctx * 2 + sec) * 2
    other_page = (ctx * 2 + 1 - sec) * 2
    wanted_pages = (own_page, own_page + 1, other_page, other_page + 1)

    def seek(block, found):
        page = page_ref[block]
        return tuple(
            jnp.where(page == wanted, block, old) for wanted, old in zip(wanted_pages, found)
        )

    found = lax.fori_loop(0, page_ref.shape[0], seek, (jnp.int32(0),) * 4)

    pick = lax.broadcasted_iota(jnp.int32, (4 * PAGE, 1), 0)
    source = pick % PAGE
    for i in range(4):
        source = source + jnp.where(pick // PAGE == i, found[i] * PAGE, 0)
    picked = jnp.zeros((4 * PAGE, 2 * HEAD), jnp.float32)
    for i, way in enumerate(near + far):
        held = chip_of(*way) * 2 * TOK + in_chip[:, : 2 * TOK]
        chosen = jnp.where(source == held, 1.0, 0.0).astype(jnp.bfloat16)
        rows = slice(i % 4 * CHIP + 2 * TOK, (i % 4 + 1) * CHIP)
        picked = picked + mm(chosen, (near_keys, far_keys)[i // 4][rows, :])
    picked = picked.astype(jnp.bfloat16).reshape(4, PAGE, 2 * HEAD)
    page_out[...] = picked[2:]
    page_copy = remote(page_out, page_in, p_send, p_recv, partner)
    page_copy.start()
    width = 2 * HEAD
    pages_ref[:, :, pl.ds(pl.multiple_of(sec * width, width), width)] = picked[:2]

    scores[...] = score(0, 1, 0)
    lax.fori_loop(0, blocks, functools.partial(step, 1), 0)
    for g in range(GROUP):
        a = acc[g * TOK : (g + 1) * TOK, :]
        fill_ref[:, g * HEAD : (g + 1) * HEAD] = (a[:, :HEAD] / a[:, HEAD:]).astype(jnp.bfloat16)

    page_copy.wait_recv()
    pages_ref[:, :, pl.ds(pl.multiple_of((1 - sec) * width, width), width)] = page_in[...]

    page_copy.wait_send()
    send_dq.wait_send()
    send_dkv.wait_send()
    for piece in (0, 1):
        for dx, dz in near[1:] + far:
            chip_copy(piece, dx, dz).wait_send()
        for dx, dz in near + far:
            core_copy(piece, dx, dz).wait_send()


def on_device(*args):
    offset = np.arange(TOK)[:, None]
    half = THETA ** (-np.arange(HEAD // 2) * 2.0 / HEAD)
    freq = np.concatenate([half, half]).astype(np.float32)
    angles = offset * freq.astype(np.float64)[None, :]
    any_spec = pl.BlockSpec(memory_space=pl.ANY)
    smem = pl.BlockSpec(memory_space=pltpu.SMEM)
    vmem = pl.BlockSpec(memory_space=pltpu.VMEM)
    bf16 = jnp.bfloat16
    dma = pltpu.SemaphoreType.DMA
    return pl.pallas_call(
        kernel,
        out_shape=(
            jax.ShapeDtypeStruct((TOK, GROUP * HEAD), bf16),
            jax.ShapeDtypeStruct((2, PAGE, 4 * HEAD), bf16),
            jax.ShapeDtypeStruct((ROWS, STEPS, 2 * GROUP * HEAD), bf16),
        ),
        in_specs=[any_spec, any_spec, any_spec, smem, smem, any_spec, any_spec, any_spec, smem]
        + [vmem] * 3,
        out_specs=(vmem,) * 3,
        scratch_shapes=[
            pltpu.VMEM((4 * CHIP, 2 * HEAD), bf16),
            pltpu.VMEM((4 * CHIP, 2 * HEAD), bf16),
            pltpu.VMEM((TOK, GROUP * HEAD), bf16),
            pltpu.VMEM((TOK, 2 * HEAD), bf16),
            pltpu.VMEM((GROUP * TOK, 2 * HEAD), bf16),
            pltpu.VMEM((GROUP * TOK, 2 * HEAD), jnp.float32),
            pltpu.VMEM((GROUP * TOK, 1), jnp.float32),
            pltpu.VMEM((8, CHIP), jnp.float32),
            pltpu.VMEM((BLOCK, CHIP), jnp.float32),
            pltpu.VMEM((2, ROWS, STEPS, GROUP * HEAD), bf16),
            pltpu.VMEM((2, ROWS, STEPS, 2 * HEAD), bf16),
            pltpu.VMEM((ROWS, SLOTS, 4 * HEAD), bf16),
            pltpu.VMEM((2, ROWS * STEPS * GROUP, HEAD), bf16),
            pltpu.VMEM((2, ROWS * STEPS * GROUP, HEAD), bf16),
            pltpu.VMEM((2, ROWS * STEPS * GROUP, 1), jnp.float32),
            pltpu.VMEM((2, ROWS * STEPS * GROUP, 1), jnp.float32),
            pltpu.VMEM((2, ROWS * STEPS * GROUP, HEAD), jnp.float32),
            pltpu.VMEM((2, PAGE, 2 * HEAD), bf16),
            pltpu.VMEM((2, PAGE, 2 * HEAD), bf16),
            dma((5,)),
            dma((ROWS,)),
            dma((2, 2, 4)),
            dma((2, 2, 4)),
            dma((2, 2, 4)),
            dma((2, 2, 4)),
            dma((2,)),
            dma((2,)),
            dma,
            dma,
        ],
        compiler_params=pltpu.CompilerParams(
            collective_id=0, has_side_effects=True, vmem_limit_bytes=58 * 2**20
        ),
        cost_estimate=pl.CostEstimate(
            flops=10 * 2**30, bytes_accessed=10 * 2**20, transcendentals=2**24
        ),
    )(
        *args,
        jnp.asarray(np.cos(angles).astype(np.float32)),
        jnp.asarray(np.sin(angles).astype(np.float32)),
        jnp.asarray(np.tile(freq[None, :], (8, 1))),
    )


def solution(mesh):
    in_specs = (
        P("ctx", ("tensor", "section")),
        P("ctx", ("tensor", "section")),
        P("ctx", ("tensor", "section")),
        P(),
        P(),
        P("ctx", None, ("tensor", "section")),
        P("ctx", None, ("tensor", "section")),
        P(("ctx", "section"), None, "tensor"),
        P(("ctx", "section")),
    )
    out_specs = (
        P("ctx", ("tensor", "section")),
        P(("ctx", "section"), None, "tensor"),
        P(("ctx", "section"), None, "tensor"),
    )
    return jax.shard_map(
        on_device, mesh=mesh, in_specs=in_specs, out_specs=out_specs, check_vma=False
    )
```

```python
import math

import jax
import jax.numpy as jnp
import numpy as np
from jax import lax
from jax.experimental import pallas as pl
from jax.experimental.pallas import tpu as pltpu
from jax.sharding import PartitionSpec as P

HEAD = 128
GROUP = 8
PAGE = 64
TOK = 256
CHIP = 4 * TOK
ROWS = 8
STEPS = 4
SLOTS = 1024
BLOCK = 512
NEG = -1e30
FAR = 1 << 30
SCALE = math.log2(math.e) / math.sqrt(HEAD)
THETA = 500000.0
MESH = pl.DeviceIdType.MESH
NT = (((1,), (1,)), ((), ()))


def mm(a, b):
    return jnp.dot(a, b, preferred_element_type=jnp.float32)


def mm_nt(a, b):
    return lax.dot_general(a, b, NT, preferred_element_type=jnp.float32)


def rotate(x, cosine, sine):
    return x * cosine + pltpu.roll(x, 64, 1) * sine


def kernel(
    sq_hbm, skv_hbm, ekv_hbm, start_ref, page_ref, dq_hbm, dkv_hbm, cache_hbm, len_ref,
    cos_ref, sin_ref, freq_ref,
    fill_ref, pages_ref, step_ref,
    near_keys, far_keys, sq, skv, qs, acc, top, bias, scores, dq, dkv, cache, qd, od, d_top, d_total, d_acc,
    page_out, page_in,
    load_sem, cache_sem, c_send, c_recv, s_send, s_recv,
    d_send, d_recv, p_send, p_recv,
):
    ctx = lax.axis_index("ctx")
    sec = lax.axis_index("section")
    core = ctx % 2
    z = (ctx // 2) % 4
    x = ctx // 8
    sibling = {"ctx": x * 8 + z * 2 + 1 - core}
    partner = {"section": 1 - sec}
    start = start_ref[0]

    def chip_of(dx, dz):
        column = x if dx == 0 else 1 - x
        return column * 4 + (z + dz) % 4

    near = ((0, 0), (1, 0), (0, 1), (0, 3))
    far = ((0, 2), (1, 1), (1, 3), (1, 2))

    def place(dx, dz, piece, other_core=0):
        ref, ways = (near_keys, near) if (dx, dz) in near else (far_keys, far)
        return ref.at[pl.ds(ways.index((dx, dz)) * CHIP + (2 * piece + other_core) * TOK, TOK)]

    def remote(src, dst, send, recv, device):
        return pltpu.make_async_remote_copy(
            src_ref=src, dst_ref=dst, send_sem=send, recv_sem=recv,
            device_id=device, device_id_type=MESH,
        )

    def peer(dx, dz):
        return {"ctx": chip_of(dx, dz) * 2 + core}

    def chip_copy(piece, dx, dz):
        back = (4 - dz) % 4
        return remote(
            place(0, 0, piece), place(dx, back, piece),
            c_send.at[piece, dx, dz], c_recv.at[piece, dx, back], peer(dx, dz),
        )

    def onward_copy(piece, dx, dz):
        source, target = ((0, 2), (1, 2)) if dx else ((1, 0), (1, (4 - dz) % 4))
        return remote(
            place(*source, piece), place(*target, piece),
            c_send.at[piece, 1, dz], c_recv.at[piece, 1, target[1]], peer(dx, 0 if dx else dz),
        )

    def chip_arrival(piece, dx, dz):
        ref = place(dx, dz, piece)
        return remote(ref, ref, c_send.at[piece, dx, dz], c_recv.at[piece, dx, dz], peer(dx, dz))

    def core_copy(piece, dx, dz):
        return remote(
            place(dx, dz, piece), place(dx, dz, piece, 1),
            s_send.at[piece, dx, dz], s_recv.at[piece, dx, dz], sibling,
        )

    def pass_on(ways):
        for dx, dz in ways:
            for piece in (0, 1):
                chip_arrival(piece, dx, dz).wait_recv()
                core_copy(piece, dx, dz).start()

    def from_sibling(ways):
        for dx, dz in ways:
            for piece in (0, 1):
                core_copy(piece, dx, dz).wait_recv()

    barrier = pltpu.get_barrier_semaphore()
    direct = near[1:] + far[:1]
    passed = ((0, 1), (0, 3), (1, 2))
    for device in [peer(dx, dz) for dx, dz in direct] + [sibling, partner]:
        pl.semaphore_signal(barrier, inc=1, device_id=device, device_id_type=MESH)

    load_e = pltpu.make_async_copy(ekv_hbm, place(0, 0, 0), load_sem.at[0])
    load_kv = pltpu.make_async_copy(skv_hbm, skv, load_sem.at[1])
    load_q = pltpu.make_async_copy(sq_hbm, sq, load_sem.at[2])
    load_e.start()
    load_kv.start()
    load_q.start()
    mine = pl.ds(sec * ROWS, ROWS)
    other = pl.ds((1 - sec) * ROWS, ROWS)
    load_dq = pltpu.make_async_copy(dq_hbm.at[mine], dq.at[sec], load_sem.at[3])
    load_dkv = pltpu.make_async_copy(dkv_hbm.at[mine], dkv.at[sec], load_sem.at[4])
    load_dq.start()
    load_dkv.start()

    def cache_copy(row):
        return pltpu.make_async_copy(cache_hbm.at[row], cache.at[row], cache_sem.at[row])

    for row in range(ROWS):
        cache_copy(row).start()

    lane = lax.broadcasted_iota(jnp.int32, (1, HEAD), 1)
    sign = jnp.where(lane < HEAD // 2, -1.0, 1.0)
    freq = freq_ref[0:1, :]
    first_angle = (start + ctx * TOK).astype(jnp.float32) * freq_ref[...]
    base_cos = jnp.cos(first_angle)[0:1]
    base_sin = jnp.sin(first_angle)[0:1]
    cosine = cos_ref[...] * base_cos - sin_ref[...] * base_sin
    sine = (sin_ref[...] * base_cos + cos_ref[...] * base_sin) * sign

    load_kv.wait()
    turned = rotate(skv[:, :HEAD].astype(jnp.float32), cosine, sine).astype(jnp.bfloat16)
    fresh_rows = slice(2 * TOK, 3 * TOK)
    near_keys[fresh_rows, :HEAD] = turned
    near_keys[fresh_rows, HEAD:] = skv[:, HEAD:]

    load_e.wait()
    pl.semaphore_wait(barrier, 6)
    send_dq = remote(dq_hbm.at[other], dq.at[sec], d_send.at[0], d_recv.at[0], partner)
    send_dkv = remote(dkv_hbm.at[other], dkv.at[sec], d_send.at[1], d_recv.at[1], partner)
    send_dkv.start()
    send_dq.start()
    for piece in (0, 1):
        for dx, dz in near[1:]:
            chip_copy(piece, dx, dz).start()
        core_copy(piece, 0, 0).start()
    for piece in (0, 1):
        chip_copy(piece, 0, 2).start()

    load_q.wait()
    for g in range(GROUP):
        part = sq[:, g * HEAD : (g + 1) * HEAD].astype(jnp.float32)
        scaled = rotate(part, cosine, sine).astype(jnp.bfloat16).astype(jnp.float32) * SCALE
        high = scaled.astype(jnp.bfloat16)
        low = (scaled - high.astype(jnp.float32)).astype(jnp.bfloat16)
        qs[g * TOK : (g + 1) * TOK, :] = jnp.concatenate([high, low], 1)

    load_dq.wait()
    load_dkv.wait()
    remote(dkv_hbm.at[other], dkv.at[1 - sec], d_send.at[1], d_recv.at[1], partner).wait_recv()
    remote(dq_hbm.at[other], dq.at[1 - sec], d_send.at[0], d_recv.at[0], partner).wait_recv()
    line = lax.broadcasted_iota(jnp.int32, (ROWS * STEPS, HEAD), 0)
    position = line % STEPS
    for row in range(ROWS):
        position = position + jnp.where(line // STEPS == row, len_ref[row], 0)
    angle = position.astype(jnp.float32) * freq
    step_cos = jnp.cos(angle)
    step_sin = jnp.sin(angle) * sign
    count = ROWS * STEPS * GROUP
    to_line = lax.broadcasted_iota(jnp.int32, (count, count), 0)
    from_line = lax.broadcasted_iota(jnp.int32, (count, count), 1)
    per_row = STEPS * GROUP
    wanted = (
        (to_line // STEPS) % GROUP * (ROWS * STEPS)
        + to_line // per_row * STEPS
        + to_line % STEPS
    )
    permute = jnp.where(wanted == from_line, 1.0, 0.0).astype(jnp.bfloat16)
    q_line = lax.broadcasted_iota(jnp.int32, (count, ROWS * STEPS), 0)
    k_line = lax.broadcasted_iota(jnp.int32, (count, ROWS * STEPS), 1)
    fresh_ok = (q_line // per_row == k_line // STEPS) & (k_line % STEPS <= q_line % STEPS)
    slot = lax.broadcasted_iota(jnp.int32, (1, SLOTS), 1)
    for h in range(2):
        lines = dq[h].astype(jnp.float32).reshape(ROWS * STEPS, GROUP * HEAD)
        parts = [
            rotate(lines[:, g * HEAD : (g + 1) * HEAD], step_cos, step_sin)
            for g in range(GROUP)
        ]
        ordered = mm(permute, jnp.concatenate(parts, 0).astype(jnp.bfloat16))
        ordered = ordered.astype(jnp.bfloat16)
        qd[h] = ordered
        fresh = dkv[h].astype(jnp.float32).reshape(ROWS * STEPS, 2 * HEAD)
        step_key = rotate(fresh[:, :HEAD], step_cos, step_sin).astype(jnp.bfloat16)
        s = jnp.where(fresh_ok, mm_nt(ordered, step_key) * SCALE, NEG)
        m = jnp.max(s, -1, keepdims=True)
        p = jnp.exp2(s - m)
        d_top[h] = m
        d_total[h] = jnp.sum(p, -1, keepdims=True)
        d_acc[h] = mm(p.astype(jnp.bfloat16), fresh[:, HEAD:].astype(jnp.bfloat16))

    def decode_rows(n, carry):
        pairs = []
        for i in range(2):
            row = 2 * n + i
            lines = pl.ds(pl.multiple_of(row * per_row, per_row), per_row)
            for h in range(2):
                s = mm_nt(qd[h, lines, :], cache[row, :, h * 256 : h * 256 + 128])
                pairs.append((row, h, lines, s))
        weights = []
        for row, h, lines, s in pairs:
            s = jnp.where(slot < len_ref[row], s * SCALE, NEG)
            m0 = d_top[h, lines, :]
            m = jnp.maximum(m0, jnp.max(s, -1, keepdims=True))
            p = jnp.exp2(s - m)
            factor = jnp.exp2(m0 - m)
            total = d_total[h, lines, :] * factor + jnp.sum(p, -1, keepdims=True)
            weights.append((p.astype(jnp.bfloat16), factor, total))
        for (row, h, lines, _), (p, factor, total) in zip(pairs, weights):
            mixed = d_acc[h, lines, :] * factor + mm(p, cache[row, :, h * 256 + 128 : (h + 1) * 256])
            od[h, lines, :] = (mixed / total).astype(jnp.bfloat16)
        return carry

    for row in range(ROWS):
        cache_copy(row).wait()
    lax.fori_loop(0, ROWS // 2, decode_rows, 0)
    pass_on(((1, 0),))
    for piece in (0, 1):
        for dz in (1, 3):
            onward_copy(piece, 0, dz).start()
    for h in range(2):
        back = lax.dot_general(
            permute, od[h], (((0,), (0,)), ((), ())), preferred_element_type=jnp.float32
        )
        for g in range(GROUP):
            lines = back[g * ROWS * STEPS : (g + 1) * ROWS * STEPS]
            lanes = slice((h * GROUP + g) * HEAD, (h * GROUP + g + 1) * HEAD)
            step_ref[:, :, lanes] = lines.reshape(ROWS, STEPS, HEAD).astype(jnp.bfloat16)

    key_lane = lax.broadcasted_iota(jnp.int32, (1, CHIP), 1)
    in_core = key_lane % (2 * TOK) // TOK
    in_chip = (core + in_core - 2 * core * in_core) * TOK + key_lane % TOK
    own_chip = chip_of(0, 0)
    for i, way in enumerate(near + far):
        chip = chip_of(*way)
        earlier = jnp.where(chip * 2 * TOK + in_chip < start, 0.0, NEG)
        fresh = jnp.where(own_chip >= chip, 0.0, NEG)
        bias[i : i + 1, :] = jnp.where(key_lane < 2 * TOK, earlier, fresh)
    own_limit = jnp.where(key_lane < 2 * TOK, -1, own_chip * 2 * TOK + in_chip)
    token = ctx * TOK + lax.broadcasted_iota(jnp.int32, (2 * BLOCK, 1), 0) % TOK
    ones = jnp.ones((CHIP, HEAD), jnp.bfloat16)

    def rows_of(i):
        return (near_keys, far_keys)[i // 4], slice(i % 4 * CHIP, (i % 4 + 1) * CHIP)

    def attend(chips, size, event=None):
        blocks = GROUP * TOK // size

        def lines_of(block):
            return pl.ds(pl.multiple_of(block * size, size), size)

        def score(block, i):
            ref, rows = rows_of(i)
            key = ref[rows, :HEAD]
            s = mm_nt(qs[lines_of(block), :], jnp.concatenate([key, key], 1)) + bias[i : i + 1, :]
            return jnp.where(own_limit <= token[:size], s, NEG) if i == 0 else s

        def step(block, carry):
            if event is not None:
                pl.when(block == 2)(event)
            lines = lines_of(block)
            m, a = top[lines, :], acc[lines, :]
            s = scores[:size, :]
            for i in chips:
                if i != chips[-1]:
                    following = score(block, i + 1)
                else:
                    scores[:size, :] = score((block + 1) % blocks, chips[0])
                higher = jnp.maximum(m, jnp.max(s, -1, keepdims=True))
                p = jnp.exp2(s - higher)
                ref, rows = rows_of(i)
                a = a * jnp.exp2(m - higher) + mm(
                    p.astype(jnp.bfloat16), jnp.concatenate([ref[rows, HEAD:], ones], 1)
                )
                m = higher
                s = following if i != chips[-1] else None
            top[lines, :], acc[lines, :] = m, a
            return carry

        scores[:size, :] = score(0, chips[0])
        lax.fori_loop(0, blocks, step, 0)

    acc[...] = jnp.zeros_like(acc)
    top[...] = jnp.full_like(top, NEG)
    from_sibling(near[:1])
    attend((0,), 2 * BLOCK)
    pass_on(near[2:])
    from_sibling(near[1:])

    def send_across():
        pass_on(far[:1])
        for piece in (0, 1):
            onward_copy(piece, 1, 2).start()

    attend((1, 2, 3), BLOCK, send_across)
    pass_on(far[1:3])
    from_sibling(far[:3])
    attend((4, 5, 6), BLOCK)
    pass_on(far[3:])
    from_sibling(far[3:])

    own_page = (ctx * 2 + sec) * 2
    other_page = (ctx * 2 + 1 - sec) * 2
    wanted_pages = (own_page, own_page + 1, other_page, other_page + 1)

    def seek(block, found):
        page = page_ref[block]
        return tuple(
            jnp.where(page == wanted, block, old) for wanted, old in zip(wanted_pages, found)
        )

    found = lax.fori_loop(0, page_ref.shape[0], seek, (jnp.int32(0),) * 4)

    pick = lax.broadcasted_iota(jnp.int32, (4 * PAGE, 1), 0)
    source = pick % PAGE
    for i in range(4):
        source = source + jnp.where(pick // PAGE == i, found[i] * PAGE, 0)
    picked = jnp.zeros((4 * PAGE, 2 * HEAD), jnp.float32)
    for i, way in enumerate(near + far):
        held = chip_of(*way) * 2 * TOK + in_chip[:, : 2 * TOK]
        chosen = jnp.where(source == held, 1.0, 0.0).astype(jnp.bfloat16)
        rows = slice(i % 4 * CHIP + 2 * TOK, (i % 4 + 1) * CHIP)
        picked = picked + mm(chosen, (near_keys, far_keys)[i // 4][rows, :])
    picked = picked.astype(jnp.bfloat16).reshape(4, PAGE, 2 * HEAD)
    page_out[...] = picked[2:]
    page_copy = remote(page_out, page_in, p_send, p_recv, partner)
    page_copy.start()
    width = 2 * HEAD
    pages_ref[:, :, pl.ds(pl.multiple_of(sec * width, width), width)] = picked[:2]

    attend((7,), 2 * BLOCK)
    for g in range(GROUP):
        a = acc[g * TOK : (g + 1) * TOK, :]
        fill_ref[:, g * HEAD : (g + 1) * HEAD] = (a[:, :HEAD] / a[:, HEAD:]).astype(jnp.bfloat16)

    page_copy.wait_recv()
    pages_ref[:, :, pl.ds(pl.multiple_of((1 - sec) * width, width), width)] = page_in[...]

    page_copy.wait_send()
    send_dq.wait_send()
    send_dkv.wait_send()
    for piece in (0, 1):
        for dx, dz in direct:
            chip_copy(piece, dx, dz).wait_send()
        for dx, dz in passed:
            onward_copy(piece, dx, dz).wait_send()
        for dx, dz in near + far:
            core_copy(piece, dx, dz).wait_send()


def store(*refs):
    for source, target in zip(refs[:3], refs[3:]):
        target[...] = source[...]


def on_device(*args):
    offset = np.arange(TOK)[:, None]
    half = THETA ** (-np.arange(HEAD // 2) * 2.0 / HEAD)
    freq = np.concatenate([half, half]).astype(np.float32)
    angles = offset * freq.astype(np.float64)[None, :]
    any_spec = pl.BlockSpec(memory_space=pl.ANY)
    smem = pl.BlockSpec(memory_space=pltpu.SMEM)
    vmem = pl.BlockSpec(memory_space=pltpu.VMEM)
    bf16 = jnp.bfloat16
    dma = pltpu.SemaphoreType.DMA
    shapes = (
        jax.ShapeDtypeStruct((TOK, GROUP * HEAD), bf16),
        jax.ShapeDtypeStruct((2, PAGE, 4 * HEAD), bf16),
        jax.ShapeDtypeStruct((ROWS, STEPS, 2 * GROUP * HEAD), bf16),
    )
    results = pl.pallas_call(
        kernel,
        out_shape=shapes,
        in_specs=[any_spec, any_spec, any_spec, smem, smem, any_spec, any_spec, any_spec, smem]
        + [vmem] * 3,
        out_specs=(vmem,) * 3,
        scratch_shapes=[
            pltpu.VMEM((4 * CHIP, 2 * HEAD), bf16),
            pltpu.VMEM((4 * CHIP, 2 * HEAD), bf16),
            pltpu.VMEM((TOK, GROUP * HEAD), bf16),
            pltpu.VMEM((TOK, 2 * HEAD), bf16),
            pltpu.VMEM((GROUP * TOK, 2 * HEAD), bf16),
            pltpu.VMEM((GROUP * TOK, 2 * HEAD), jnp.float32),
            pltpu.VMEM((GROUP * TOK, 1), jnp.float32),
            pltpu.VMEM((8, CHIP), jnp.float32),
            pltpu.VMEM((2 * BLOCK, CHIP), jnp.float32),
            pltpu.VMEM((2, ROWS, STEPS, GROUP * HEAD), bf16),
            pltpu.VMEM((2, ROWS, STEPS, 2 * HEAD), bf16),
            pltpu.VMEM((ROWS, SLOTS, 4 * HEAD), bf16),
            pltpu.VMEM((2, ROWS * STEPS * GROUP, HEAD), bf16),
            pltpu.VMEM((2, ROWS * STEPS * GROUP, HEAD), bf16),
            pltpu.VMEM((2, ROWS * STEPS * GROUP, 1), jnp.float32),
            pltpu.VMEM((2, ROWS * STEPS * GROUP, 1), jnp.float32),
            pltpu.VMEM((2, ROWS * STEPS * GROUP, HEAD), jnp.float32),
            pltpu.VMEM((2, PAGE, 2 * HEAD), bf16),
            pltpu.VMEM((2, PAGE, 2 * HEAD), bf16),
            dma((5,)),
            dma((ROWS,)),
            dma((2, 2, 4)),
            dma((2, 2, 4)),
            dma((2, 2, 4)),
            dma((2, 2, 4)),
            dma((2,)),
            dma((2,)),
            dma,
            dma,
        ],
        compiler_params=pltpu.CompilerParams(
            collective_id=0, has_side_effects=True, vmem_limit_bytes=58 * 2**20
        ),
        cost_estimate=pl.CostEstimate(
            flops=10 * 2**30, bytes_accessed=10 * 2**20, transcendentals=2**24
        ),
    )(
        *args,
        jnp.asarray(np.cos(angles).astype(np.float32)),
        jnp.asarray(np.sin(angles).astype(np.float32)),
        jnp.asarray(np.tile(freq[None, :], (8, 1))),
    )
    return pl.pallas_call(
        store,
        out_shape=shapes,
        in_specs=[vmem] * 3,
        out_specs=(vmem,) * 3,
    )(*results)


def solution(mesh):
    in_specs = (
        P("ctx", ("tensor", "section")),
        P("ctx", ("tensor", "section")),
        P("ctx", ("tensor", "section")),
        P(),
        P(),
        P("ctx", None, ("tensor", "section")),
        P("ctx", None, ("tensor", "section")),
        P(("ctx", "section"), None, "tensor"),
        P(("ctx", "section")),
    )
    out_specs = (
        P("ctx", ("tensor", "section")),
        P(("ctx", "section"), None, "tensor"),
        P(("ctx", "section"), None, "tensor"),
    )
    return jax.shard_map(
        on_device, mesh=mesh, in_specs=in_specs, out_specs=out_specs, check_vma=False
    )
```

```python
import math

import jax
import jax.numpy as jnp
import numpy as np
from jax import lax
from jax.experimental import pallas as pl
from jax.experimental.pallas import tpu as pltpu
from jax.sharding import PartitionSpec as P

HEAD = 128
GROUP = 8
PAGE = 64
TOK = 256
CHIP = 4 * TOK
ROWS = 8
STEPS = 4
SLOTS = 1024
BLOCK = 512
NEG = -1e30
FAR = 1 << 30
SCALE = math.log2(math.e) / math.sqrt(HEAD)
THETA = 500000.0
MESH = pl.DeviceIdType.MESH
NT = (((1,), (1,)), ((), ()))


def mm(a, b):
    return jnp.dot(a, b, preferred_element_type=jnp.float32)


def mm_nt(a, b):
    return lax.dot_general(a, b, NT, preferred_element_type=jnp.float32)


def rotate(x, cosine, sine):
    return x * cosine + pltpu.roll(x, 64, 1) * sine


def kernel(
    sq_hbm, skv_hbm, ekv_hbm, start_ref, page_ref, dq_hbm, dkv_hbm, cache_hbm, len_ref,
    cos_ref, sin_ref, freq_ref,
    fill_ref, pages_ref, step_ref,
    near_keys, far_keys, sq, skv, qs, acc, top, bias, scores, dq, dkv, cache, qd, od, d_top, d_total, d_acc,
    page_out, page_in,
    load_sem, cache_sem, c_send, c_recv, s_send, s_recv,
    d_send, d_recv, p_send, p_recv,
):
    ctx = lax.axis_index("ctx")
    sec = lax.axis_index("section")
    core = ctx % 2
    z = (ctx // 2) % 4
    x = ctx // 8
    sibling = {"ctx": x * 8 + z * 2 + 1 - core}
    partner = {"section": 1 - sec}
    start = start_ref[0]

    def chip_of(dx, dz):
        column = x if dx == 0 else 1 - x
        return column * 4 + (z + dz) % 4

    near = ((0, 0), (1, 0), (0, 1), (0, 3))
    far = ((0, 2), (1, 1), (1, 3), (1, 2))

    def place(dx, dz, piece, other_core=0):
        ref, ways = (near_keys, near) if (dx, dz) in near else (far_keys, far)
        return ref.at[pl.ds(ways.index((dx, dz)) * CHIP + (2 * piece + other_core) * TOK, TOK)]

    def remote(src, dst, send, recv, device):
        return pltpu.make_async_remote_copy(
            src_ref=src, dst_ref=dst, send_sem=send, recv_sem=recv,
            device_id=device, device_id_type=MESH,
        )

    def peer(dx, dz):
        return {"ctx": chip_of(dx, dz) * 2 + core}

    def chip_copy(piece, dx, dz):
        back = (4 - dz) % 4
        return remote(
            place(0, 0, piece), place(dx, back, piece),
            c_send.at[piece, dx, dz], c_recv.at[piece, dx, back], peer(dx, dz),
        )

    def onward_copy(piece, dx, dz):
        source, target = ((0, 2), (1, 2)) if dx else ((1, 0), (1, (4 - dz) % 4))
        return remote(
            place(*source, piece), place(*target, piece),
            c_send.at[piece, 1, dz], c_recv.at[piece, 1, target[1]], peer(dx, 0 if dx else dz),
        )

    def chip_arrival(piece, dx, dz):
        ref = place(dx, dz, piece)
        return remote(ref, ref, c_send.at[piece, dx, dz], c_recv.at[piece, dx, dz], peer(dx, dz))

    def core_copy(piece, dx, dz):
        return remote(
            place(dx, dz, piece), place(dx, dz, piece, 1),
            s_send.at[piece, dx, dz], s_recv.at[piece, dx, dz], sibling,
        )

    def pass_on(ways):
        for dx, dz in ways:
            for piece in (0, 1):
                chip_arrival(piece, dx, dz).wait_recv()
                core_copy(piece, dx, dz).start()

    def from_sibling(ways):
        for dx, dz in ways:
            for piece in (0, 1):
                core_copy(piece, dx, dz).wait_recv()

    barrier = pltpu.get_barrier_semaphore()
    direct = near[1:] + far[:1]
    passed = ((0, 1), (0, 3), (1, 2))
    for device in [peer(dx, dz) for dx, dz in direct] + [sibling, partner]:
        pl.semaphore_signal(barrier, inc=1, device_id=device, device_id_type=MESH)

    load_e = pltpu.make_async_copy(ekv_hbm, place(0, 0, 0), load_sem.at[0])
    load_kv = pltpu.make_async_copy(skv_hbm, skv, load_sem.at[1])
    load_q = pltpu.make_async_copy(sq_hbm, sq, load_sem.at[2])
    load_e.start()
    load_kv.start()
    load_q.start()
    mine = pl.ds(sec * ROWS, ROWS)
    other = pl.ds((1 - sec) * ROWS, ROWS)
    load_dq = pltpu.make_async_copy(dq_hbm.at[mine], dq.at[sec], load_sem.at[3])
    load_dkv = pltpu.make_async_copy(dkv_hbm.at[mine], dkv.at[sec], load_sem.at[4])
    load_dq.start()
    load_dkv.start()

    def cache_copy(row):
        return pltpu.make_async_copy(cache_hbm.at[row], cache.at[row], cache_sem.at[row])

    for row in range(ROWS):
        cache_copy(row).start()

    def send(piece):
        for dx, dz in near[1:]:
            chip_copy(piece, dx, dz).start()
        core_copy(piece, 0, 0).start()

    send_dq = remote(dq_hbm.at[other], dq.at[sec], d_send.at[0], d_recv.at[0], partner)
    send_dkv = remote(dkv_hbm.at[other], dkv.at[sec], d_send.at[1], d_recv.at[1], partner)
    load_e.wait()
    pl.semaphore_wait(barrier, 6)
    send_dkv.start()
    send_dq.start()
    send(0)

    lane = lax.broadcasted_iota(jnp.int32, (1, HEAD), 1)
    sign = jnp.where(lane < HEAD // 2, -1.0, 1.0)
    freq = freq_ref[0:1, :]
    first_angle = (start + ctx * TOK).astype(jnp.float32) * freq_ref[...]
    base_cos = jnp.cos(first_angle)[0:1]
    base_sin = jnp.sin(first_angle)[0:1]
    cosine = cos_ref[...] * base_cos - sin_ref[...] * base_sin
    sine = (sin_ref[...] * base_cos + cos_ref[...] * base_sin) * sign

    load_kv.wait()
    turned = rotate(skv[:, :HEAD].astype(jnp.float32), cosine, sine).astype(jnp.bfloat16)
    fresh_rows = slice(2 * TOK, 3 * TOK)
    near_keys[fresh_rows, :HEAD] = turned
    near_keys[fresh_rows, HEAD:] = skv[:, HEAD:]

    send(1)
    for piece in (0, 1):
        chip_copy(piece, 0, 2).start()

    load_q.wait()
    for g in range(GROUP):
        part = sq[:, g * HEAD : (g + 1) * HEAD].astype(jnp.float32)
        scaled = rotate(part, cosine, sine).astype(jnp.bfloat16).astype(jnp.float32) * SCALE
        high = scaled.astype(jnp.bfloat16)
        low = (scaled - high.astype(jnp.float32)).astype(jnp.bfloat16)
        qs[g * TOK : (g + 1) * TOK, :] = jnp.concatenate([high, low], 1)

    load_dq.wait()
    load_dkv.wait()
    remote(dkv_hbm.at[other], dkv.at[1 - sec], d_send.at[1], d_recv.at[1], partner).wait_recv()
    remote(dq_hbm.at[other], dq.at[1 - sec], d_send.at[0], d_recv.at[0], partner).wait_recv()
    line = lax.broadcasted_iota(jnp.int32, (ROWS * STEPS, HEAD), 0)
    position = line % STEPS
    for row in range(ROWS):
        position = position + jnp.where(line // STEPS == row, len_ref[row], 0)
    angle = position.astype(jnp.float32) * freq
    step_cos = jnp.cos(angle)
    step_sin = jnp.sin(angle) * sign
    count = ROWS * STEPS * GROUP
    to_line = lax.broadcasted_iota(jnp.int32, (count, count), 0)
    from_line = lax.broadcasted_iota(jnp.int32, (count, count), 1)
    per_row = STEPS * GROUP
    wanted = (
        (to_line // STEPS) % GROUP * (ROWS * STEPS)
        + to_line // per_row * STEPS
        + to_line % STEPS
    )
    permute = jnp.where(wanted == from_line, 1.0, 0.0).astype(jnp.bfloat16)
    q_line = lax.broadcasted_iota(jnp.int32, (count, ROWS * STEPS), 0)
    k_line = lax.broadcasted_iota(jnp.int32, (count, ROWS * STEPS), 1)
    fresh_ok = (q_line // per_row == k_line // STEPS) & (k_line % STEPS <= q_line % STEPS)
    slot = lax.broadcasted_iota(jnp.int32, (1, SLOTS), 1)
    for h in range(2):
        lines = dq[h].astype(jnp.float32).reshape(ROWS * STEPS, GROUP * HEAD)
        parts = [
            rotate(lines[:, g * HEAD : (g + 1) * HEAD], step_cos, step_sin)
            for g in range(GROUP)
        ]
        ordered = mm(permute, jnp.concatenate(parts, 0).astype(jnp.bfloat16))
        ordered = ordered.astype(jnp.bfloat16)
        qd[h] = ordered
        fresh = dkv[h].astype(jnp.float32).reshape(ROWS * STEPS, 2 * HEAD)
        step_key = rotate(fresh[:, :HEAD], step_cos, step_sin).astype(jnp.bfloat16)
        s = jnp.where(fresh_ok, mm_nt(ordered, step_key) * SCALE, NEG)
        m = jnp.max(s, -1, keepdims=True)
        p = jnp.exp2(s - m)
        d_top[h] = m
        d_total[h] = jnp.sum(p, -1, keepdims=True)
        d_acc[h] = mm(p.astype(jnp.bfloat16), fresh[:, HEAD:].astype(jnp.bfloat16))

    def decode_rows(n, carry):
        pairs = []
        for i in range(2):
            row = 2 * n + i
            lines = pl.ds(pl.multiple_of(row * per_row, per_row), per_row)
            for h in range(2):
                s = mm_nt(qd[h, lines, :], cache[row, :, h * 256 : h * 256 + 128])
                pairs.append((row, h, lines, s))
        weights = []
        for row, h, lines, s in pairs:
            s = jnp.where(slot < len_ref[row], s * SCALE, NEG)
            m0 = d_top[h, lines, :]
            m = jnp.maximum(m0, jnp.max(s, -1, keepdims=True))
            p = jnp.exp2(s - m)
            factor = jnp.exp2(m0 - m)
            total = d_total[h, lines, :] * factor + jnp.sum(p, -1, keepdims=True)
            weights.append((p.astype(jnp.bfloat16), factor, total))
        for (row, h, lines, _), (p, factor, total) in zip(pairs, weights):
            mixed = d_acc[h, lines, :] * factor + mm(p, cache[row, :, h * 256 + 128 : (h + 1) * 256])
            od[h, lines, :] = (mixed / total).astype(jnp.bfloat16)
        return carry

    for row in range(ROWS):
        cache_copy(row).wait()
    lax.fori_loop(0, ROWS // 2, decode_rows, 0)
    pass_on(((1, 0),))
    for piece in (0, 1):
        for dz in (1, 3):
            onward_copy(piece, 0, dz).start()
    for h in range(2):
        back = lax.dot_general(
            permute, od[h], (((0,), (0,)), ((), ())), preferred_element_type=jnp.float32
        )
        for g in range(GROUP):
            lines = back[g * ROWS * STEPS : (g + 1) * ROWS * STEPS]
            lanes = slice((h * GROUP + g) * HEAD, (h * GROUP + g + 1) * HEAD)
            step_ref[:, :, lanes] = lines.reshape(ROWS, STEPS, HEAD).astype(jnp.bfloat16)

    key_lane = lax.broadcasted_iota(jnp.int32, (1, CHIP), 1)
    in_core = key_lane % (2 * TOK) // TOK
    in_chip = (core + in_core - 2 * core * in_core) * TOK + key_lane % TOK
    own_chip = chip_of(0, 0)
    for i, way in enumerate(near + far):
        chip = chip_of(*way)
        earlier = jnp.where(chip * 2 * TOK + in_chip < start, 0.0, NEG)
        fresh = jnp.where(own_chip >= chip, 0.0, NEG)
        bias[i : i + 1, :] = jnp.where(key_lane < 2 * TOK, earlier, fresh)
    own_limit = jnp.where(key_lane < 2 * TOK, -1, own_chip * 2 * TOK + in_chip)
    token = ctx * TOK + lax.broadcasted_iota(jnp.int32, (2 * BLOCK, 1), 0) % TOK
    ones = jnp.ones((CHIP, HEAD), jnp.bfloat16)

    def rows_of(i):
        return (near_keys, far_keys)[i // 4], slice(i % 4 * CHIP, (i % 4 + 1) * CHIP)

    def attend(chips, size, event=None):
        blocks = GROUP * TOK // size

        def lines_of(block):
            return pl.ds(pl.multiple_of(block * size, size), size)

        def score(block, i):
            ref, rows = rows_of(i)
            key = ref[rows, :HEAD]
            s = mm_nt(qs[lines_of(block), :], jnp.concatenate([key, key], 1)) + bias[i : i + 1, :]
            return jnp.where(own_limit <= token[:size], s, NEG) if i == 0 else s

        def step(block, carry):
            if event is not None:
                pl.when(block == 2)(event)
            lines = lines_of(block)
            m, a = top[lines, :], acc[lines, :]
            s = scores[:size, :]
            for i in chips:
                if i != chips[-1]:
                    following = score(block, i + 1)
                else:
                    scores[:size, :] = score((block + 1) % blocks, chips[0])
                higher = jnp.maximum(m, jnp.max(s, -1, keepdims=True))
                p = jnp.exp2(s - higher)
                ref, rows = rows_of(i)
                a = a * jnp.exp2(m - higher) + mm(
                    p.astype(jnp.bfloat16), jnp.concatenate([ref[rows, HEAD:], ones], 1)
                )
                m = higher
                s = following if i != chips[-1] else None
            top[lines, :], acc[lines, :] = m, a
            return carry

        scores[:size, :] = score(0, chips[0])
        lax.fori_loop(0, blocks, step, 0)

    acc[...] = jnp.zeros_like(acc)
    top[...] = jnp.full_like(top, NEG)
    from_sibling(near[:1])
    attend((0,), 2 * BLOCK)
    pass_on(near[2:])
    from_sibling(near[1:])

    def send_across():
        pass_on(far[:1])
        for piece in (0, 1):
            onward_copy(piece, 1, 2).start()

    attend((1, 2, 3), BLOCK, send_across)
    pass_on(far[1:3])
    from_sibling(far[:3])
    attend((4, 5, 6), BLOCK)
    pass_on(far[3:])
    from_sibling(far[3:])

    own_page = (ctx * 2 + sec) * 2
    other_page = (ctx * 2 + 1 - sec) * 2
    wanted_pages = (own_page, own_page + 1, other_page, other_page + 1)

    def seek(block, found):
        page = page_ref[block]
        return tuple(
            jnp.where(page == wanted, block, old) for wanted, old in zip(wanted_pages, found)
        )

    found = lax.fori_loop(0, page_ref.shape[0], seek, (jnp.int32(0),) * 4)

    pick = lax.broadcasted_iota(jnp.int32, (4 * PAGE, 1), 0)
    source = pick % PAGE
    for i in range(4):
        source = source + jnp.where(pick // PAGE == i, found[i] * PAGE, 0)
    picked = jnp.zeros((4 * PAGE, 2 * HEAD), jnp.float32)
    for i, way in enumerate(near + far):
        held = chip_of(*way) * 2 * TOK + in_chip[:, : 2 * TOK]
        chosen = jnp.where(source == held, 1.0, 0.0).astype(jnp.bfloat16)
        rows = slice(i % 4 * CHIP + 2 * TOK, (i % 4 + 1) * CHIP)
        picked = picked + mm(chosen, (near_keys, far_keys)[i // 4][rows, :])
    picked = picked.astype(jnp.bfloat16).reshape(4, PAGE, 2 * HEAD)
    page_out[...] = picked[2:]
    page_copy = remote(page_out, page_in, p_send, p_recv, partner)
    page_copy.start()
    width = 2 * HEAD
    pages_ref[:, :, pl.ds(pl.multiple_of(sec * width, width), width)] = picked[:2]

    attend((7,), 2 * BLOCK)
    for g in range(GROUP):
        a = acc[g * TOK : (g + 1) * TOK, :]
        fill_ref[:, g * HEAD : (g + 1) * HEAD] = (a[:, :HEAD] / a[:, HEAD:]).astype(jnp.bfloat16)

    page_copy.wait_recv()
    pages_ref[:, :, pl.ds(pl.multiple_of((1 - sec) * width, width), width)] = page_in[...]

    page_copy.wait_send()
    send_dq.wait_send()
    send_dkv.wait_send()
    for piece in (0, 1):
        for dx, dz in direct:
            chip_copy(piece, dx, dz).wait_send()
        for dx, dz in passed:
            onward_copy(piece, dx, dz).wait_send()
        for dx, dz in near + far:
            core_copy(piece, dx, dz).wait_send()


def store(*refs):
    for source, target in zip(refs[:3], refs[3:]):
        target[...] = source[...]


def on_device(*args):
    offset = np.arange(TOK)[:, None]
    half = THETA ** (-np.arange(HEAD // 2) * 2.0 / HEAD)
    freq = np.concatenate([half, half]).astype(np.float32)
    angles = offset * freq.astype(np.float64)[None, :]
    any_spec = pl.BlockSpec(memory_space=pl.ANY)
    smem = pl.BlockSpec(memory_space=pltpu.SMEM)
    vmem = pl.BlockSpec(memory_space=pltpu.VMEM)
    bf16 = jnp.bfloat16
    dma = pltpu.SemaphoreType.DMA
    shapes = (
        jax.ShapeDtypeStruct((TOK, GROUP * HEAD), bf16),
        jax.ShapeDtypeStruct((2, PAGE, 4 * HEAD), bf16),
        jax.ShapeDtypeStruct((ROWS, STEPS, 2 * GROUP * HEAD), bf16),
    )
    results = pl.pallas_call(
        kernel,
        out_shape=shapes,
        in_specs=[any_spec, any_spec, any_spec, smem, smem, any_spec, any_spec, any_spec, smem]
        + [vmem] * 3,
        out_specs=(vmem,) * 3,
        scratch_shapes=[
            pltpu.VMEM((4 * CHIP, 2 * HEAD), bf16),
            pltpu.VMEM((4 * CHIP, 2 * HEAD), bf16),
            pltpu.VMEM((TOK, GROUP * HEAD), bf16),
            pltpu.VMEM((TOK, 2 * HEAD), bf16),
            pltpu.VMEM((GROUP * TOK, 2 * HEAD), bf16),
            pltpu.VMEM((GROUP * TOK, 2 * HEAD), jnp.float32),
            pltpu.VMEM((GROUP * TOK, 1), jnp.float32),
            pltpu.VMEM((8, CHIP), jnp.float32),
            pltpu.VMEM((2 * BLOCK, CHIP), jnp.float32),
            pltpu.VMEM((2, ROWS, STEPS, GROUP * HEAD), bf16),
            pltpu.VMEM((2, ROWS, STEPS, 2 * HEAD), bf16),
            pltpu.VMEM((ROWS, SLOTS, 4 * HEAD), bf16),
            pltpu.VMEM((2, ROWS * STEPS * GROUP, HEAD), bf16),
            pltpu.VMEM((2, ROWS * STEPS * GROUP, HEAD), bf16),
            pltpu.VMEM((2, ROWS * STEPS * GROUP, 1), jnp.float32),
            pltpu.VMEM((2, ROWS * STEPS * GROUP, 1), jnp.float32),
            pltpu.VMEM((2, ROWS * STEPS * GROUP, HEAD), jnp.float32),
            pltpu.VMEM((2, PAGE, 2 * HEAD), bf16),
            pltpu.VMEM((2, PAGE, 2 * HEAD), bf16),
            dma((5,)),
            dma((ROWS,)),
            dma((2, 2, 4)),
            dma((2, 2, 4)),
            dma((2, 2, 4)),
            dma((2, 2, 4)),
            dma((2,)),
            dma((2,)),
            dma,
            dma,
        ],
        compiler_params=pltpu.CompilerParams(
            collective_id=0, has_side_effects=True, vmem_limit_bytes=58 * 2**20
        ),
        cost_estimate=pl.CostEstimate(
            flops=10 * 2**30, bytes_accessed=10 * 2**20, transcendentals=2**24
        ),
    )(
        *args,
        jnp.asarray(np.cos(angles).astype(np.float32)),
        jnp.asarray(np.sin(angles).astype(np.float32)),
        jnp.asarray(np.tile(freq[None, :], (8, 1))),
    )
    return pl.pallas_call(
        store,
        out_shape=shapes,
        in_specs=[vmem] * 3,
        out_specs=(vmem,) * 3,
    )(*results)


def solution(mesh):
    in_specs = (
        P("ctx", ("tensor", "section")),
        P("ctx", ("tensor", "section")),
        P("ctx", ("tensor", "section")),
        P(),
        P(),
        P("ctx", None, ("tensor", "section")),
        P("ctx", None, ("tensor", "section")),
        P(("ctx", "section"), None, "tensor"),
        P(("ctx", "section")),
    )
    out_specs = (
        P("ctx", ("tensor", "section")),
        P(("ctx", "section"), None, "tensor"),
        P(("ctx", "section"), None, "tensor"),
    )
    return jax.shard_map(
        on_device, mesh=mesh, in_specs=in_specs, out_specs=out_specs, check_vma=False
    )
```

```python
import math

import jax
import jax.numpy as jnp
import numpy as np
from jax import lax
from jax.experimental import pallas as pl
from jax.experimental.pallas import tpu as pltpu
from jax.sharding import PartitionSpec as P

HEAD = 128
GROUP = 8
PAGE = 64
TOK = 256
CHIP = 4 * TOK
ROWS = 8
STEPS = 4
SLOTS = 1024
BLOCK = 512
NEG = -1e30
FAR = 1 << 30
SCALE = math.log2(math.e) / math.sqrt(HEAD)
THETA = 500000.0
MESH = pl.DeviceIdType.MESH
NT = (((1,), (1,)), ((), ()))


def mm(a, b):
    return jnp.dot(a, b, preferred_element_type=jnp.float32)


def mm_nt(a, b):
    return lax.dot_general(a, b, NT, preferred_element_type=jnp.float32)


def rotate(x, cosine, sine):
    return x * cosine + pltpu.roll(x, 64, 1) * sine


def kernel(
    sq_hbm, skv_hbm, ekv_hbm, start_ref, page_ref, dq_hbm, dkv_hbm, cache_hbm, len_ref,
    cos_ref, sin_ref, freq_ref,
    fill_ref, pages_ref, step_ref,
    near_keys, far_keys, sq, skv, qs, acc, top, bias, scores, dq, dkv, cache, qd, od, d_top, d_total, d_acc,
    page_out, page_in,
    load_sem, cache_sem, c_send, c_recv, s_send, s_recv,
    d_send, d_recv, p_send, p_recv,
):
    ctx = lax.axis_index("ctx")
    sec = lax.axis_index("section")
    core = ctx % 2
    z = (ctx // 2) % 4
    x = ctx // 8
    sibling = {"ctx": x * 8 + z * 2 + 1 - core}
    partner = {"section": 1 - sec}
    start = start_ref[0]

    def chip_of(dx, dz):
        column = x if dx == 0 else 1 - x
        return column * 4 + (z + dz) % 4

    near = ((0, 0), (1, 0), (0, 1), (0, 3))
    far = ((0, 2), (1, 1), (1, 3), (1, 2))

    def place(dx, dz, piece, other_core=0):
        ref, ways = (near_keys, near) if (dx, dz) in near else (far_keys, far)
        return ref.at[pl.ds(ways.index((dx, dz)) * CHIP + (2 * piece + other_core) * TOK, TOK)]

    def remote(src, dst, send, recv, device):
        return pltpu.make_async_remote_copy(
            src_ref=src, dst_ref=dst, send_sem=send, recv_sem=recv,
            device_id=device, device_id_type=MESH,
        )

    def peer(dx, dz):
        return {"ctx": chip_of(dx, dz) * 2 + core}

    def chip_copy(piece, dx, dz):
        back = (4 - dz) % 4
        return remote(
            place(0, 0, piece), place(dx, back, piece),
            c_send.at[piece, dx, dz], c_recv.at[piece, dx, back], peer(dx, dz),
        )

    def onward_copy(piece, dx, dz):
        source, target = ((0, 2), (1, 2)) if dx else ((1, 0), (1, (4 - dz) % 4))
        return remote(
            place(*source, piece), place(*target, piece),
            c_send.at[piece, 1, dz], c_recv.at[piece, 1, target[1]], peer(dx, 0 if dx else dz),
        )

    def chip_arrival(piece, dx, dz):
        ref = place(dx, dz, piece)
        return remote(ref, ref, c_send.at[piece, dx, dz], c_recv.at[piece, dx, dz], peer(dx, dz))

    def core_copy(piece, dx, dz):
        return remote(
            place(dx, dz, piece), place(dx, dz, piece, 1),
            s_send.at[piece, dx, dz], s_recv.at[piece, dx, dz], sibling,
        )

    def pass_on(ways):
        for dx, dz in ways:
            for piece in (0, 1):
                chip_arrival(piece, dx, dz).wait_recv()
                core_copy(piece, dx, dz).start()

    def from_sibling(ways):
        for dx, dz in ways:
            for piece in (0, 1):
                core_copy(piece, dx, dz).wait_recv()

    barrier = pltpu.get_barrier_semaphore()
    direct = near[1:] + far[:1]
    passed = ((0, 1), (0, 3), (1, 2))
    for device in [peer(dx, dz) for dx, dz in direct] + [sibling, partner]:
        pl.semaphore_signal(barrier, inc=1, device_id=device, device_id_type=MESH)

    load_e = pltpu.make_async_copy(ekv_hbm, place(0, 0, 0), load_sem.at[0])
    load_kv = pltpu.make_async_copy(skv_hbm, skv, load_sem.at[1])
    load_q = pltpu.make_async_copy(sq_hbm, sq, load_sem.at[2])
    load_e.start()
    load_kv.start()
    load_q.start()
    mine = pl.ds(sec * ROWS, ROWS)
    other = pl.ds((1 - sec) * ROWS, ROWS)
    load_dq = pltpu.make_async_copy(dq_hbm.at[mine], dq.at[sec], load_sem.at[3])
    load_dkv = pltpu.make_async_copy(dkv_hbm.at[mine], dkv.at[sec], load_sem.at[4])
    load_dq.start()
    load_dkv.start()

    def cache_copy(row):
        return pltpu.make_async_copy(cache_hbm.at[row], cache.at[row], cache_sem.at[row])

    for row in range(ROWS):
        cache_copy(row).start()

    lane = lax.broadcasted_iota(jnp.int32, (1, HEAD), 1)
    sign = jnp.where(lane < HEAD // 2, -1.0, 1.0)
    freq = freq_ref[0:1, :]
    first_angle = (start + ctx * TOK).astype(jnp.float32) * freq_ref[...]
    base_cos = jnp.cos(first_angle)[0:1]
    base_sin = jnp.sin(first_angle)[0:1]
    cosine = cos_ref[...] * base_cos - sin_ref[...] * base_sin
    sine = (sin_ref[...] * base_cos + cos_ref[...] * base_sin) * sign

    load_kv.wait()
    turned = rotate(skv[:, :HEAD].astype(jnp.float32), cosine, sine).astype(jnp.bfloat16)
    fresh_rows = slice(2 * TOK, 3 * TOK)
    near_keys[fresh_rows, :HEAD] = turned
    near_keys[fresh_rows, HEAD:] = skv[:, HEAD:]

    load_e.wait()
    pl.semaphore_wait(barrier, 6)
    send_dq = remote(dq_hbm.at[other], dq.at[sec], d_send.at[0], d_recv.at[0], partner)
    send_dkv = remote(dkv_hbm.at[other], dkv.at[sec], d_send.at[1], d_recv.at[1], partner)
    send_dkv.start()
    send_dq.start()
    for piece in (0, 1):
        for dx, dz in near[1:]:
            chip_copy(piece, dx, dz).start()
        core_copy(piece, 0, 0).start()
    for piece in (0, 1):
        chip_copy(piece, 0, 2).start()

    load_q.wait()
    for g in range(GROUP):
        part = sq[:, g * HEAD : (g + 1) * HEAD].astype(jnp.float32)
        scaled = rotate(part, cosine, sine).astype(jnp.bfloat16).astype(jnp.float32) * SCALE
        high = scaled.astype(jnp.bfloat16)
        low = (scaled - high.astype(jnp.float32)).astype(jnp.bfloat16)
        qs[g * TOK : (g + 1) * TOK, :] = jnp.concatenate([high, low], 1)

    load_dq.wait()
    load_dkv.wait()
    remote(dkv_hbm.at[other], dkv.at[1 - sec], d_send.at[1], d_recv.at[1], partner).wait_recv()
    remote(dq_hbm.at[other], dq.at[1 - sec], d_send.at[0], d_recv.at[0], partner).wait_recv()
    line = lax.broadcasted_iota(jnp.int32, (ROWS * STEPS, HEAD), 0)
    position = line % STEPS
    for row in range(ROWS):
        position = position + jnp.where(line // STEPS == row, len_ref[row], 0)
    angle = position.astype(jnp.float32) * freq
    step_cos = jnp.cos(angle)
    step_sin = jnp.sin(angle) * sign
    count = ROWS * STEPS * GROUP
    to_line = lax.broadcasted_iota(jnp.int32, (count, count), 0)
    from_line = lax.broadcasted_iota(jnp.int32, (count, count), 1)
    per_row = STEPS * GROUP
    wanted = (
        (to_line // STEPS) % GROUP * (ROWS * STEPS)
        + to_line // per_row * STEPS
        + to_line % STEPS
    )
    permute = jnp.where(wanted == from_line, 1.0, 0.0).astype(jnp.bfloat16)
    q_line = lax.broadcasted_iota(jnp.int32, (count, ROWS * STEPS), 0)
    k_line = lax.broadcasted_iota(jnp.int32, (count, ROWS * STEPS), 1)
    fresh_ok = (q_line // per_row == k_line // STEPS) & (k_line % STEPS <= q_line % STEPS)
    slot = lax.broadcasted_iota(jnp.int32, (1, SLOTS), 1)
    for h in range(2):
        lines = dq[h].astype(jnp.float32).reshape(ROWS * STEPS, GROUP * HEAD)
        parts = [
            rotate(lines[:, g * HEAD : (g + 1) * HEAD], step_cos, step_sin)
            for g in range(GROUP)
        ]
        ordered = mm(permute, jnp.concatenate(parts, 0).astype(jnp.bfloat16))
        ordered = ordered.astype(jnp.bfloat16)
        qd[h] = ordered
        fresh = dkv[h].astype(jnp.float32).reshape(ROWS * STEPS, 2 * HEAD)
        step_key = rotate(fresh[:, :HEAD], step_cos, step_sin).astype(jnp.bfloat16)
        s = jnp.where(fresh_ok, mm_nt(ordered, step_key) * SCALE, NEG)
        m = jnp.max(s, -1, keepdims=True)
        p = jnp.exp2(s - m)
        d_top[h] = m
        d_total[h] = jnp.sum(p, -1, keepdims=True)
        d_acc[h] = mm(p.astype(jnp.bfloat16), fresh[:, HEAD:].astype(jnp.bfloat16))

    def decode_rows(n, carry):
        pairs = []
        for i in range(2):
            row = 2 * n + i
            lines = pl.ds(pl.multiple_of(row * per_row, per_row), per_row)
            for h in range(2):
                s = mm_nt(qd[h, lines, :], cache[row, :, h * 256 : h * 256 + 128])
                pairs.append((row, h, lines, s))
        weights = []
        for row, h, lines, s in pairs:
            s = jnp.where(slot < len_ref[row], s * SCALE, NEG)
            m0 = d_top[h, lines, :]
            m = jnp.maximum(m0, jnp.max(s, -1, keepdims=True))
            p = jnp.exp2(s - m)
            factor = jnp.exp2(m0 - m)
            total = d_total[h, lines, :] * factor + jnp.sum(p, -1, keepdims=True)
            weights.append((p.astype(jnp.bfloat16), factor, total))
        for (row, h, lines, _), (p, factor, total) in zip(pairs, weights):
            mixed = d_acc[h, lines, :] * factor + mm(p, cache[row, :, h * 256 + 128 : (h + 1) * 256])
            od[h, lines, :] = (mixed / total).astype(jnp.bfloat16)
        return carry

    for row in range(ROWS):
        cache_copy(row).wait()
    lax.fori_loop(0, ROWS // 2, decode_rows, 0)
    pass_on(((1, 0),))
    for piece in (0, 1):
        for dz in (1, 3):
            onward_copy(piece, 0, dz).start()
    for h in range(2):
        back = lax.dot_general(
            permute, od[h], (((0,), (0,)), ((), ())), preferred_element_type=jnp.float32
        )
        for g in range(GROUP):
            lines = back[g * ROWS * STEPS : (g + 1) * ROWS * STEPS]
            lanes = slice((h * GROUP + g) * HEAD, (h * GROUP + g + 1) * HEAD)
            step_ref[:, :, lanes] = lines.reshape(ROWS, STEPS, HEAD).astype(jnp.bfloat16)

    key_lane = lax.broadcasted_iota(jnp.int32, (1, CHIP), 1)
    in_core = key_lane % (2 * TOK) // TOK
    in_chip = (core + in_core - 2 * core * in_core) * TOK + key_lane % TOK
    own_chip = chip_of(0, 0)
    for i, way in enumerate(near + far):
        chip = chip_of(*way)
        earlier = jnp.where(chip * 2 * TOK + in_chip < start, 0.0, NEG)
        fresh = jnp.where(own_chip >= chip, 0.0, NEG)
        bias[i : i + 1, :] = jnp.where(key_lane < 2 * TOK, earlier, fresh)
    own_limit = jnp.where(key_lane < 2 * TOK, -1, own_chip * 2 * TOK + in_chip)
    token = ctx * TOK + lax.broadcasted_iota(jnp.int32, (2 * BLOCK, 1), 0) % TOK
    ones = jnp.ones((CHIP, HEAD), jnp.bfloat16)

    def rows_of(i):
        return (near_keys, far_keys)[i // 4], slice(i % 4 * CHIP, (i % 4 + 1) * CHIP)

    def attend(chips, size, event=None, when=2):
        blocks = GROUP * TOK // size

        def lines_of(block):
            return pl.ds(pl.multiple_of(block * size, size), size)

        def score(block, i):
            ref, rows = rows_of(i)
            key = ref[rows, :HEAD]
            s = mm_nt(qs[lines_of(block), :], jnp.concatenate([key, key], 1)) + bias[i : i + 1, :]
            return jnp.where(own_limit <= token[:size], s, NEG) if i == 0 else s

        def step(block, carry):
            if event is not None:
                pl.when(block == when)(event)
            lines = lines_of(block)
            m, a = top[lines, :], acc[lines, :]
            s = scores[:size, :]
            for i in chips:
                if i != chips[-1]:
                    following = score(block, i + 1)
                else:
                    scores[:size, :] = score((block + 1) % blocks, chips[0])
                higher = jnp.maximum(m, jnp.max(s, -1, keepdims=True))
                p = jnp.exp2(s - higher)
                ref, rows = rows_of(i)
                a = a * jnp.exp2(m - higher) + mm(
                    p.astype(jnp.bfloat16), jnp.concatenate([ref[rows, HEAD:], ones], 1)
                )
                m = higher
                s = following if i != chips[-1] else None
            top[lines, :], acc[lines, :] = m, a
            return carry

        scores[:size, :] = score(0, chips[0])
        lax.fori_loop(0, blocks, step, 0)

    acc[...] = jnp.zeros_like(acc)
    top[...] = jnp.full_like(top, NEG)
    from_sibling(near[:1])
    attend((0,), 2 * BLOCK, lambda: pass_on(near[2:]), 1)
    from_sibling(near[1:])

    def send_across():
        pass_on(far[:1])
        for piece in (0, 1):
            onward_copy(piece, 1, 2).start()

    attend((1, 2, 3), BLOCK, send_across)
    pass_on(far[1:3])
    from_sibling(far[:3])
    attend((4, 5, 6), BLOCK, lambda: pass_on(far[3:]))
    from_sibling(far[3:])

    own_page = (ctx * 2 + sec) * 2
    other_page = (ctx * 2 + 1 - sec) * 2
    wanted_pages = (own_page, own_page + 1, other_page, other_page + 1)

    def seek(block, found):
        page = page_ref[block]
        return tuple(
            jnp.where(page == wanted, block, old) for wanted, old in zip(wanted_pages, found)
        )

    found = lax.fori_loop(0, page_ref.shape[0], seek, (jnp.int32(0),) * 4)

    pick = lax.broadcasted_iota(jnp.int32, (4 * PAGE, 1), 0)
    source = pick % PAGE
    for i in range(4):
        source = source + jnp.where(pick // PAGE == i, found[i] * PAGE, 0)
    picked = jnp.zeros((4 * PAGE, 2 * HEAD), jnp.float32)
    for i, way in enumerate(near + far):
        held = chip_of(*way) * 2 * TOK + in_chip[:, : 2 * TOK]
        chosen = jnp.where(source == held, 1.0, 0.0).astype(jnp.bfloat16)
        rows = slice(i % 4 * CHIP + 2 * TOK, (i % 4 + 1) * CHIP)
        picked = picked + mm(chosen, (near_keys, far_keys)[i // 4][rows, :])
    picked = picked.astype(jnp.bfloat16).reshape(4, PAGE, 2 * HEAD)
    page_out[...] = picked[2:]
    page_copy = remote(page_out, page_in, p_send, p_recv, partner)
    page_copy.start()
    width = 2 * HEAD
    pages_ref[:, :, pl.ds(pl.multiple_of(sec * width, width), width)] = picked[:2]

    attend((7,), 2 * BLOCK)
    for g in range(GROUP):
        a = acc[g * TOK : (g + 1) * TOK, :]
        fill_ref[:, g * HEAD : (g + 1) * HEAD] = (a[:, :HEAD] / a[:, HEAD:]).astype(jnp.bfloat16)

    page_copy.wait_recv()
    pages_ref[:, :, pl.ds(pl.multiple_of((1 - sec) * width, width), width)] = page_in[...]

    page_copy.wait_send()
    send_dq.wait_send()
    send_dkv.wait_send()
    for piece in (0, 1):
        for dx, dz in direct:
            chip_copy(piece, dx, dz).wait_send()
        for dx, dz in passed:
            onward_copy(piece, dx, dz).wait_send()
        for dx, dz in near + far:
            core_copy(piece, dx, dz).wait_send()


def store(*refs):
    for source, target in zip(refs[:3], refs[3:]):
        target[...] = source[...]


def on_device(*args):
    offset = np.arange(TOK)[:, None]
    half = THETA ** (-np.arange(HEAD // 2) * 2.0 / HEAD)
    freq = np.concatenate([half, half]).astype(np.float32)
    angles = offset * freq.astype(np.float64)[None, :]
    any_spec = pl.BlockSpec(memory_space=pl.ANY)
    smem = pl.BlockSpec(memory_space=pltpu.SMEM)
    vmem = pl.BlockSpec(memory_space=pltpu.VMEM)
    bf16 = jnp.bfloat16
    dma = pltpu.SemaphoreType.DMA
    shapes = (
        jax.ShapeDtypeStruct((TOK, GROUP * HEAD), bf16),
        jax.ShapeDtypeStruct((2, PAGE, 4 * HEAD), bf16),
        jax.ShapeDtypeStruct((ROWS, STEPS, 2 * GROUP * HEAD), bf16),
    )
    results = pl.pallas_call(
        kernel,
        out_shape=shapes,
        in_specs=[any_spec, any_spec, any_spec, smem, smem, any_spec, any_spec, any_spec, smem]
        + [vmem] * 3,
        out_specs=(vmem,) * 3,
        scratch_shapes=[
            pltpu.VMEM((4 * CHIP, 2 * HEAD), bf16),
            pltpu.VMEM((4 * CHIP, 2 * HEAD), bf16),
            pltpu.VMEM((TOK, GROUP * HEAD), bf16),
            pltpu.VMEM((TOK, 2 * HEAD), bf16),
            pltpu.VMEM((GROUP * TOK, 2 * HEAD), bf16),
            pltpu.VMEM((GROUP * TOK, 2 * HEAD), jnp.float32),
            pltpu.VMEM((GROUP * TOK, 1), jnp.float32),
            pltpu.VMEM((8, CHIP), jnp.float32),
            pltpu.VMEM((2 * BLOCK, CHIP), jnp.float32),
            pltpu.VMEM((2, ROWS, STEPS, GROUP * HEAD), bf16),
            pltpu.VMEM((2, ROWS, STEPS, 2 * HEAD), bf16),
            pltpu.VMEM((ROWS, SLOTS, 4 * HEAD), bf16),
            pltpu.VMEM((2, ROWS * STEPS * GROUP, HEAD), bf16),
            pltpu.VMEM((2, ROWS * STEPS * GROUP, HEAD), bf16),
            pltpu.VMEM((2, ROWS * STEPS * GROUP, 1), jnp.float32),
            pltpu.VMEM((2, ROWS * STEPS * GROUP, 1), jnp.float32),
            pltpu.VMEM((2, ROWS * STEPS * GROUP, HEAD), jnp.float32),
            pltpu.VMEM((2, PAGE, 2 * HEAD), bf16),
            pltpu.VMEM((2, PAGE, 2 * HEAD), bf16),
            dma((5,)),
            dma((ROWS,)),
            dma((2, 2, 4)),
            dma((2, 2, 4)),
            dma((2, 2, 4)),
            dma((2, 2, 4)),
            dma((2,)),
            dma((2,)),
            dma,
            dma,
        ],
        compiler_params=pltpu.CompilerParams(
            collective_id=0, has_side_effects=True, vmem_limit_bytes=58 * 2**20
        ),
        cost_estimate=pl.CostEstimate(
            flops=10 * 2**30, bytes_accessed=10 * 2**20, transcendentals=2**24
        ),
    )(
        *args,
        jnp.asarray(np.cos(angles).astype(np.float32)),
        jnp.asarray(np.sin(angles).astype(np.float32)),
        jnp.asarray(np.tile(freq[None, :], (8, 1))),
    )
    return pl.pallas_call(
        store,
        out_shape=shapes,
        in_specs=[vmem] * 3,
        out_specs=(vmem,) * 3,
    )(*results)


def solution(mesh):
    in_specs = (
        P("ctx", ("tensor", "section")),
        P("ctx", ("tensor", "section")),
        P("ctx", ("tensor", "section")),
        P(),
        P(),
        P("ctx", None, ("tensor", "section")),
        P("ctx", None, ("tensor", "section")),
        P(("ctx", "section"), None, "tensor"),
        P(("ctx", "section")),
    )
    out_specs = (
        P("ctx", ("tensor", "section")),
        P(("ctx", "section"), None, "tensor"),
        P(("ctx", "section"), None, "tensor"),
    )
    return jax.shard_map(
        on_device, mesh=mesh, in_specs=in_specs, out_specs=out_specs, check_vma=False
    )
```
